128 devices in a mesh: section: 8 (over x, core), sector: 16 (over z, y).
Axes of the slice: x: 4, y: 4, z: 4, core: 2. Of those that a mesh axis runs over, the one named last changes fastest.
Arguments:
- wavefunction: bfloat16 [8, 16, 16, 256, 256], P('section', None, 'sector'), may hold values from -6 to 6
- left_env: bfloat16 [8, 14, 16, 256, 256], P('section', None, 'sector'), may hold values from -1 to 2
- right_env: bfloat16 [8, 14, 16, 256, 256], P('section', None, 'sector'), may hold values from -1 to 2
- term_table: int32 [16, 4], replicated, may hold values from 0 to 13
- source_table: int32 [16, 4], replicated, may hold values from 0 to 15
- live_sizes: int32 [8, 2, 16], P('section'), may hold values from 1 to 256, 3072 in all within a row
Outputs:
- next_basis: float32 [8, 16, 16, 256, 256], P('section', None, 'sector')
- projected: float32 [8, 3], P('section')
The draws below stay inside these ranges and needn't reach their ends.
Inputs may be any that keep to these rules, and one draw needn't show every extreme that they name: `live_sizes`: each row of 16 live sizes sums to 3072 and its largest entry is exactly 256.
All inputs are finite; a program needn't handle non-finite values.
Results may differ from the reference program's by a relative error of at most 0.008.
Values may be sent and summed in bfloat16 or wider, within the bound.
No kernel may reach another device: no remote copies, remote signals or barrier semaphores. Data moves between devices by JAX's collectives and lax.ppermute only.
A program may use at most 128 MiB of HBM per device.

```python
import math
import jax
import jax.numpy as jnp
import numpy as np
from jax import lax

M = 256
W = 14
K = 4
NQ = 16
SECTIONS = 8
N_SECTION = 8


def environment_blocks(key, spread):
    shape = (SECTIONS, W, NQ, M, M)
    noise = jnp.clip(jax.random.normal(key, shape, jnp.float32), -4.0, 4.0) * spread
    diagonal = jnp.eye(M, dtype=jnp.float32)
    return (noise + diagonal).astype(jnp.bfloat16)


def draw_left_env(key, part):
    key = jax.random.fold_in(key, 11)
    return environment_blocks(key, 1.0 / M ** 0.5)


def draw_right_env(key, part):
    key = jax.random.fold_in(key, 23)
    return environment_blocks(key, 1.0 / M ** 0.5)


def draw_source_table(key, part):
    key = jax.random.fold_in(key, 37)
    others = jax.random.randint(key, (NQ, K - 1), 0, NQ, dtype=jnp.int32)
    own = jnp.arange(NQ, dtype=jnp.int32)[:, None]
    return jnp.concatenate([own, others], axis=1)


def place_ends(array, stream_key, smallest, largest):
    longest = array.shape.index(max(array.shape))
    spots = []
    for shift in (0, 1):
        where = [jax.random.randint(jax.random.fold_in(stream_key, axis), (), 0, length) for axis, length in enumerate(array.shape)]
        where[longest] = (where[longest] + shift) % array.shape[longest]
        spots.append(tuple(where))
    return array.at[spots[0]].set(smallest).at[spots[1]].set(largest)


def block_levels(key, extent, split, least, high):
    level, own = 1.0, jax.random.fold_in(key, 6)
    for axis_at, shards_of in split:
        heights = jnp.exp(jax.random.uniform(jax.random.fold_in(own, axis_at), (shards_of,), jnp.float32, least / len(split), high / len(split)))
        level = level * jnp.repeat(heights, extent[axis_at] // shards_of).reshape([-1 if axis == axis_at else 1 for axis in range(len(extent))])
    return level


def length_profile(count, total, most, slope):
    weights = [(1 << 20) // math.isqrt(standing ** slope) + 1 for standing in range(2, count + 1)]
    rest, given = total - most - (count - 1), [1] * (count - 1)
    while rest > 0:
        movable = [i for i in range(count - 1) if given[i] < most]
        whole, left = sum([weights[i] for i in movable]), rest
        for i in movable:
            addition = min(most - given[i], max(1, left * weights[i] // whole), rest)
            given[i] = given[i] + addition
            rest = rest - addition
    return np.array([most] + given)


def ragged_sizes(rng, count, total, most, lean):
    if count == 2:
        one = jax.random.randint(rng, (), max(1, total - most), min(most, total - 1) + 1)
        return jnp.stack([one, total - one])
    sizes = jnp.asarray(length_profile(count, total, most, lean), jnp.int32)
    couples = (count - 1) // 2
    donor, sink = sizes[1:1 + 2 * couples:2], sizes[2:2 + 2 * couples:2]
    slack = jnp.minimum(donor - 1, most - sink)
    moved = jax.random.randint(jax.random.fold_in(rng, 1), (couples,), 0, 1 << 20) % (slack + 1)
    sizes = sizes.at[1:1 + 2 * couples:2].set(donor - moved).at[2:2 + 2 * couples:2].set(sink + moved)
    return sizes[jax.random.permutation(jax.random.fold_in(rng, 2), count)]


def gaussian(rng, dims, scale, reach, shards=(), held_as=jnp.bfloat16):
    gain = block_levels(rng, dims, shards, -0.22, 0.18) if shards else 1.0
    result = jax.random.normal(rng, dims, jnp.float32) * scale * gain
    return jnp.minimum(jnp.maximum(result, -reach), reach).astype(held_as)


def setup_inputs(seed: int = 0) -> dict:
    streams_of = jax.random.split(jax.random.key(seed), 7)
    wavefunction = gaussian(streams_of[0], (SECTIONS, NQ, NQ, M, M), 1.0, 6.0, ((0, 8), (2, 16)))
    left_env = draw_left_env(jax.random.fold_in(streams_of[6], 71), 0)
    right_env = draw_right_env(jax.random.fold_in(streams_of[6], 71), 0)
    term_table = place_ends(jax.random.randint(streams_of[3], (NQ, K), 0, W), jax.random.fold_in(streams_of[3], 1), 0, W - 1).astype(jnp.int32)
    source_table = draw_source_table(jax.random.fold_in(streams_of[6], 71), 0)
    live_sizes = jax.vmap(lambda own: ragged_sizes(own, NQ, 3 * NQ * M // 4, M, 2))(jax.random.split(streams_of[5], SECTIONS * 2)).reshape((SECTIONS, 2, NQ)).astype(jnp.int32)
    return {"wavefunction": wavefunction, "left_env": left_env, "right_env": right_env, "term_table": term_table, "source_table": source_table, "live_sizes": live_sizes}


epsilon = 1e-06

def apply_operator(vector_bf, left_own, right_partner, term_table, source_table, live_mask):

    def one_row(sector):
        picked = vector_bf[source_table[sector]].astype(jnp.float32)
        right_blocks = right_partner[term_table[sector]].astype(jnp.float32)
        inner_part = jnp.einsum('kbij,kbjl->kbil', picked, right_blocks).astype(jnp.bfloat16)
        inner_part = lax.optimization_barrier(inner_part)
        left_blocks = left_own[term_table[sector], sector].astype(jnp.float32)
        return jnp.einsum('kij,kbjl->bil', left_blocks, inner_part.astype(jnp.float32))
    image = lax.map(one_row, jnp.arange(NQ, dtype=jnp.int32))
    return image * live_mask

def cell_mean(values):
    return jnp.sum(values) / jnp.float32(NQ * NQ * M * M)

def one_section(inputs, term_table, source_table):
    wave, left_own, right_partner, sizes = inputs
    positions = jnp.arange(M, dtype=jnp.int32)
    live_rows = positions[None, :] < sizes[0][:, None]
    live_cols = positions[None, :] < sizes[1][:, None]
    live_mask = (live_rows[:, None, :, None] & live_cols[None, :, None, :]).astype(jnp.float32)
    masked = wave.astype(jnp.float32) * live_mask
    first_vector = masked * lax.rsqrt(cell_mean(masked * masked) + epsilon)
    first_image = apply_operator(first_vector.astype(jnp.bfloat16), left_own, right_partner, term_table, source_table, live_mask)
    rayleigh = cell_mean(first_vector * first_image)
    residual = first_image - rayleigh * first_vector
    second_vector = residual * lax.rsqrt(cell_mean(residual * residual) + epsilon)
    second_image = apply_operator(second_vector.astype(jnp.bfloat16), left_own, right_partner, term_table, source_table, live_mask)
    upper_entry = cell_mean(first_vector * second_image)
    lower_entry = cell_mean(second_vector * second_image)
    remainder = second_image - upper_entry * first_vector - lower_entry * second_vector
    next_basis = remainder * lax.rsqrt(cell_mean(remainder * remainder) + epsilon)
    return (next_basis, jnp.stack([rayleigh, upper_entry, lower_entry]))

def reference(wavefunction, left_env, right_env, term_table, source_table, live_sizes):
    paired = right_env.reshape((N_SECTION // 2, 2) + right_env.shape[1:])
    right_partner = paired[:, ::-1].reshape(right_env.shape)
    next_basis, projected = lax.map(lambda inputs: one_section(inputs, term_table, source_table), (wavefunction, left_env, right_partner, live_sizes))
    return (next_basis, projected)
```

```python
import functools

import jax
import jax.numpy as jnp
from jax import lax
from jax.experimental import pallas as pl
from jax.experimental.pallas import tpu as pltpu
from jax.sharding import PartitionSpec as P

epsilon = 1e-06
SIDE = 4
OFFSETS = (0, 3, 1, 2)
MIB = 1 << 20


def ring(dz, dy):
    return [
        (z * SIDE + y, ((z + dz) % SIDE) * SIDE + (y + dy) % SIDE)
        for z in range(SIDE)
        for y in range(SIDE)
    ]


def along(axis, step):
    return ring(step % SIDE, 0) if axis == "z" else ring(0, step % SIDE)


def send(block, axis, step):
    return lax.ppermute(block, "sector", along(axis, step))


def gather_halves(half_a, half_b):
    tie = lax.optimization_barrier
    routes = ((half_a, "y", "z"), (half_b, "z", "y"))
    near = [send(own, first, step) for own, first, _ in routes for step in (1, -1)]
    across = [send(own, first, 2) for own, first, _ in routes]
    near = tie(tuple(near))
    low = [jnp.stack([half_a, near[0]]), jnp.stack([half_b, near[2]])]
    across = tie(tuple(across))
    high = [jnp.stack([near[1], across[0]]), jnp.stack([near[3], across[1]])]
    axes = [second for _, _, second in routes]
    back_a, ahead_a, back_b, ahead_b = tie(
        (
            send(low[0], axes[0], 1),
            send(high[0], axes[0], -1),
            send(low[1], axes[1], 1),
            send(high[1], axes[1], -1),
        )
    )
    first = (back_a, back_b), (ahead_a, ahead_b)
    pieces = []
    for i, axis in enumerate(axes):
        low_back, high_ahead = first[0][i], first[1][i]
        high_back = send(high[i], axis, 1)
        low_ahead = send(low[i], axis, -1)
        low_across = send(low_back, axis, 1)
        high_across = send(high_ahead, axis, -1)
        pieces.append(
            [
                (low[i], high[i]),
                (low_back, high_back),
                (low_ahead, high_ahead),
                (low_across, high_across),
            ]
        )
    return pieces, near


def left_sector(sector, z_at, y_at):
    z = lax.rem(sector // SIDE + OFFSETS[z_at], SIDE)
    y = lax.rem(lax.rem(sector, SIDE) + OFFSETS[y_at], SIDE)
    return z * SIDE + y


def fold(block):
    return jnp.sum(block.reshape(block.shape[0] // 8, 8, block.shape[1]), axis=0)


def dot(a, b):
    return jnp.dot(a, b, preferred_element_type=jnp.float32)


def pick_kernel(sector, terms, sizes, left, half_a, half_b, blocks, sems):
    me = sector[0]
    copies = [pltpu.make_async_copy(left.at[0, terms[k, me], 0], blocks.at[k], sems.at[k]) for k in range(4)]
    for copy in copies:
        copy.start()
    size = blocks.shape[-1]
    keep = lax.broadcasted_iota(jnp.int32, (size, size), 0) < sizes[0, 0, me]
    for k, copy in enumerate(copies):
        copy.wait()
        block = jnp.where(keep, blocks[k].astype(jnp.float32), 0.0).astype(jnp.bfloat16)
        (half_a, half_b)[k // 2][k % 2] = block


def inner_product(a, k, terms, sources, vector, right):
    return dot(vector[sources[k, a]], right[terms[k, a]]).astype(jnp.bfloat16)


def left_block(pieces, z_at, y_at, k):
    if k < 2:
        return pieces[2 * z_at + y_at // 2][y_at % 2, k]
    return pieces[len(pieces) // 2 + 2 * y_at + z_at // 2][z_at % 2, k - 2]


def row_image(a, z_at, y_at, ks, terms, sources, vector, right, pieces):
    inner = [inner_product(a, k, terms, sources, vector, right) for k in ks]
    blocks = [left_block(pieces, z_at, y_at, k) for k in ks]
    return dot(jnp.concatenate(blocks, axis=1), jnp.concatenate(inner, axis=0))


WHOLE = [(z_at, y_at) for z_at in range(3) for y_at in range(3)]
LATE = [(3, 0), (3, 1), (3, 2), (0, 3), (1, 3), (2, 3), (3, 3)]


def late_ks(z_at, y_at):
    return ((0, 1) if z_at == 3 else ()) + ((2, 3) if y_at == 3 else ())


LATE_INNER = [(at, k) for at in LATE for k in late_ks(*at)]


def spread(total):
    return jnp.broadcast_to(jnp.sum(total, keepdims=True), (1, 128))


def first_kernel(sector, terms, sources, sizes, wave, right, *refs):
    pieces, (masked, right_live, field, part, inner, sums), (image,) = refs[:12], refs[12:18], refs[18:]
    size = image.shape[-1]
    me = sector[0]
    rows = lax.broadcasted_iota(jnp.int32, (size, size), 0)
    col_keep = lax.broadcasted_iota(jnp.int32, (size, size), 1) < sizes[0, 1, me]
    zero = jnp.zeros((8, size), jnp.float32)

    def mask_right(t, carry):
        right_live[t] = jnp.where(col_keep, right[0, t, 0].astype(jnp.float32), 0.0).astype(jnp.bfloat16)
        return carry

    def mask_wave(c, ww):
        keep = (rows < sizes[0, 0, c]) & col_keep
        w = jnp.where(keep, wave[0, c, 0].astype(jnp.float32), 0.0)
        masked[c] = w.astype(jnp.bfloat16)
        return ww + fold(w * w)

    lax.fori_loop(0, right_live.shape[0], mask_right, 0)
    ww = lax.fori_loop(0, masked.shape[0], mask_wave, zero)

    some_ww, some_wy = zero, zero
    for i, (z_at, y_at) in enumerate(WHOLE):
        a = left_sector(me, z_at, y_at)
        y = row_image(a, z_at, y_at, (0, 1, 2, 3), terms, sources, masked, right_live, pieces)
        image[i] = y
        w = masked[a].astype(jnp.float32)
        some_ww += fold(w * w)
        some_wy += fold(w * y)
    for i, (z_at, y_at) in enumerate(LATE[:6]):
        a = left_sector(me, z_at, y_at)
        ks = (2, 3) if z_at == 3 else (0, 1)
        part[i] = row_image(a, z_at, y_at, ks, terms, sources, masked, right_live, pieces)
    for i, ((z_at, y_at), k) in enumerate(LATE_INNER):
        a = left_sector(me, z_at, y_at)
        inner[i] = inner_product(a, k, terms, sources, masked, right_live)

    some_ww = jnp.sum(some_ww, keepdims=True)
    some_wy = jnp.sum(some_wy, keepdims=True)
    slope = jnp.where(some_ww > 0.0, some_wy / jnp.where(some_ww > 0.0, some_ww, 1.0), 0.0)
    wu, uu = zero, zero
    for i, (z_at, y_at) in enumerate(WHOLE):
        a = left_sector(me, z_at, y_at)
        w = masked[a].astype(jnp.float32)
        u = (image[i] - slope * w).astype(jnp.bfloat16)
        field[i] = u
        u = u.astype(jnp.float32)
        wu += fold(w * u)
        uu += fold(u * u)
    slope = jnp.broadcast_to(slope, (1, 128))
    sums[...] = jnp.concatenate([spread(ww), spread(wu), spread(uu)] + [slope] * 5, axis=0)


def second_kernel(sector, terms, sources, masked, right_live, field_some, part, inner, sums_first, *refs):
    pieces, (field, image, sums) = refs[:16], refs[16:]
    size = image.shape[-1]
    me = sector[0]
    zero = jnp.zeros((8, size), jnp.float32)
    slope = sums_first[3:4, :1]
    wu, uu = zero, zero
    at = 0
    for i, (z_at, y_at) in enumerate(LATE):
        a = left_sector(me, z_at, y_at)
        ks = late_ks(z_at, y_at)
        blocks = [left_block(pieces, z_at, y_at, k) for k in ks]
        late_inner = jnp.concatenate([inner[at + j] for j in range(len(ks))], axis=0)
        at += len(ks)
        y = dot(jnp.concatenate(blocks, axis=1), late_inner)
        if i < 6:
            y += part[i]
        w = masked[a].astype(jnp.float32)
        u = (y - slope * w).astype(jnp.bfloat16)
        field[a] = u
        u = u.astype(jnp.float32)
        wu += fold(w * u)
        uu += fold(u * u)
    for i, (z_at, y_at) in enumerate(WHOLE):
        field[left_sector(me, z_at, y_at)] = field_some[i]

    wv, uv, vv = zero, zero, zero
    for z_at in range(4):
        for y_at in range(4):
            a = left_sector(me, z_at, y_at)
            v = row_image(a, z_at, y_at, (0, 1, 2, 3), terms, sources, field, right_live, pieces)
            image[a] = v
            wv += fold(masked[a].astype(jnp.float32) * v)
            uv += fold(field[a].astype(jnp.float32) * v)
            vv += fold(v * v)

    head = sums_first[...]
    block = jnp.concatenate(
        [
            head[0:1],
            head[1:2] + spread(wu),
            head[2:3] + spread(uu),
            spread(wv),
            spread(uv),
            spread(vv),
            head[3:4],
            head[3:4],
        ],
        axis=0,
    )
    sums[...] = jnp.broadcast_to(block[None], sums.shape)


def last_kernel(cells, gathered, own, masked, field, image, out, projected, weights):
    step = pl.program_id(0)

    @pl.when(step == 0)
    def _():
        g = gathered[...]
        ww, wu, uu, wv, uv, vv, slope = (g[:, j, :] for j in range(7))

        def total(values):
            return jnp.sum(values, axis=0, keepdims=True) / cells

        alpha = lax.rsqrt(total(ww) + epsilon)
        wy = wu + slope * ww
        uy = uu + slope * wu
        theta = alpha * alpha * total(wy)
        delta = theta - slope
        beta = lax.rsqrt(alpha * alpha * total(uu - 2.0 * delta * wu + delta * delta * ww) + epsilon)
        scale = alpha * beta
        upper = alpha * scale * total(wv - delta * wy)
        lower = scale * scale * total(uv - delta * uy - delta * (wv - delta * wy))
        cu = delta + lower
        cw = delta * slope - lower * delta + upper / beta
        squares = vv + cu * cu * uu + cw * cw * ww - 2.0 * (cu * uv + cw * wv - cu * cw * wu)
        gamma = lax.rsqrt(scale * scale * total(squares) + epsilon)
        factor = gamma * scale
        own_slope = own[0, 6:7, :]
        own_delta = theta - own_slope
        own_cu = own_delta + lower
        own_cw = own_delta * own_slope - lower * own_delta + upper / beta
        weights[...] = jnp.concatenate([factor, factor * own_cu, factor * own_cw], axis=0)
        lane = lax.broadcasted_iota(jnp.int32, theta.shape, 1)
        entries = jnp.where(lane == 0, theta, jnp.where(lane == 1, upper, lower))
        projected[...] = entries[:, :3]

    def wide(j):
        row = weights[j : j + 1, :]
        return jnp.concatenate([row] * (out.shape[-1] // 128), axis=1)[None]

    per_step = out.shape[1]
    here = pl.ds(step * per_step, per_step)
    out[0, :, 0] = (
        image[here] * wide(0)
        - field[here].astype(jnp.float32) * wide(1)
        - masked[here].astype(jnp.float32) * wide(2)
    )


def per_device(wavefunction, left_env, right_env, term_table, source_table, live_sizes):
    sectors, size = wavefunction.shape[1], wavefunction.shape[3]
    terms_count = left_env.shape[1]
    smem = pl.BlockSpec(memory_space=pltpu.SMEM)
    vmem = pl.BlockSpec(memory_space=pltpu.VMEM)
    bf16, f32 = jnp.bfloat16, jnp.float32
    sector = lax.axis_index("sector").astype(jnp.int32)[None]
    terms, sources = term_table.T, source_table.T

    def blocks(count, dtype):
        return jax.ShapeDtypeStruct((count, size, size), dtype)

    half_a, half_b = pl.pallas_call(
        pick_kernel,
        out_shape=(blocks(2, bf16), blocks(2, bf16)),
        in_specs=[smem, smem, smem, pl.BlockSpec(memory_space=pl.ANY)],
        out_specs=(vmem, vmem),
        scratch_shapes=[pltpu.VMEM((4, size, size), bf16), pltpu.SemaphoreType.DMA((4,))],
        compiler_params=pltpu.CompilerParams(vmem_limit_bytes=4 * MIB),
        name="pick_left",
    )(sector, terms, live_sizes, left_env)

    (pairs_a, pairs_b), near = gather_halves(half_a, half_b)
    early = [p for pairs in (pairs_a, pairs_b) for pair in pairs[:3] for p in pair]
    every = [p for pairs in (pairs_a, pairs_b) for pair in pairs for p in pair]
    count = lax.axis_size("section")
    right_env, _ = lax.optimization_barrier((right_env, near[0]))
    partner = lax.ppermute(right_env, "section", [(s, s ^ 1) for s in range(count)])

    flop = 2 * size * size * size
    masked, right_live, field_some, part, inner, sums_first = pl.pallas_call(
        first_kernel,
        out_shape=(
            blocks(sectors, bf16),
            blocks(terms_count, bf16),
            blocks(len(WHOLE), bf16),
            blocks(6, f32),
            blocks(len(LATE_INNER), bf16),
            jax.ShapeDtypeStruct((8, 128), f32),
        ),
        in_specs=[smem] * 4 + [vmem] * 14,
        out_specs=(vmem,) * 6,
        scratch_shapes=[pltpu.VMEM((len(WHOLE), size, size), f32)],
        compiler_params=pltpu.CompilerParams(vmem_limit_bytes=20 * MIB),
        cost_estimate=pl.CostEstimate(flops=112 * flop, bytes_accessed=16 * MIB, transcendentals=0),
        name="first_image",
    )(sector, terms, sources, live_sizes, wavefunction, partner, *early)

    field, image, sums = pl.pallas_call(
        second_kernel,
        out_shape=(
            blocks(sectors, bf16),
            blocks(sectors, f32),
            jax.ShapeDtypeStruct((sectors, 8, 128), f32),
        ),
        in_specs=[smem] * 3 + [vmem] * 22,
        out_specs=(vmem,) * 3,
        compiler_params=pltpu.CompilerParams(vmem_limit_bytes=20 * MIB),
        cost_estimate=pl.CostEstimate(flops=144 * flop, bytes_accessed=24 * MIB, transcendentals=0),
        name="second_image",
    )(sector, terms, sources, masked, right_live, field_some, part, inner, sums_first, *every)

    gathered = lax.all_to_all(sums, "sector", 0, 0)
    per_step = 2
    cells = float(sectors * sectors * size * size)
    next_basis, projected = pl.pallas_call(
        functools.partial(last_kernel, cells),
        grid=(sectors // per_step,),
        out_shape=(
            jax.ShapeDtypeStruct((1, sectors, 1, size, size), f32),
            jax.ShapeDtypeStruct((1, 3), f32),
        ),
        in_specs=[vmem] * 5,
        out_specs=(
            pl.BlockSpec((1, per_step, 1, size, size), lambda i: (0, i, 0, 0, 0)),
            pl.BlockSpec((1, 3), lambda i: (0, 0)),
        ),
        scratch_shapes=[pltpu.VMEM((3, 128), f32)],
        compiler_params=pltpu.CompilerParams(vmem_limit_bytes=8 * MIB),
        name="next_basis",
    )(gathered, sums, masked, field, image)
    return next_basis, projected


def solution(mesh):
    in_specs = (
        P("section", None, "sector", None, None),
        P("section", None, "sector", None, None),
        P("section", None, "sector", None, None),
        P(),
        P(),
        P("section", None, None),
    )
    out_specs = (P("section", None, "sector", None, None), P("section", None))
    return jax.shard_map(
        per_device, mesh=mesh, in_specs=in_specs, out_specs=out_specs, check_vma=False
    )
```

```python
import functools

import jax
import jax.numpy as jnp
from jax import lax
from jax.experimental import pallas as pl
from jax.experimental.pallas import tpu as pltpu
from jax.sharding import PartitionSpec as P

epsilon = 1e-06
SIDE = 4
OFFSETS = (0, 3, 1, 2)
MIB = 1 << 20


def ring(dz, dy):
    return [
        (z * SIDE + y, ((z + dz) % SIDE) * SIDE + (y + dy) % SIDE)
        for z in range(SIDE)
        for y in range(SIDE)
    ]


def along(axis, step):
    return ring(step % SIDE, 0) if axis == "z" else ring(0, step % SIDE)


def send(block, axis, step):
    return lax.ppermute(block, "sector", along(axis, step))


def after(value, *results):
    return lax.optimization_barrier((value, *results))[0]


def gather_halves(half_a, half_b):
    own = (half_a, half_b)
    first, second = ("y", "z"), ("z", "y")
    near = {(i, step): send(own[i], first[i], step) for i in range(2) for step in (1, -1)}
    across = [send(near[i, 1], first[i], 1) for i in range(2)]
    last = {(first[i], step): near[i, step] for i in range(2) for step in (1, -1)}
    last.update({(first[i], 1): across[i] for i in range(2)})
    low = [jnp.stack([own[i], near[i, 1]]) for i in range(2)]
    high = [jnp.stack([near[i, -1], across[i]]) for i in range(2)]
    low_next, high_next = {}, {}
    for i in range(2):
        for step in (1, -1):
            low_next[i, step] = send(after(low[i], last[second[i], step]), second[i], step)
    for i in range(2):
        for step in (1, -1):
            high_next[i, step] = send(after(high[i], low_next[i, step]), second[i], step)
    pieces = []
    for i in range(2):
        low_across = send(after(low_next[i, 1], high_next[i, 1]), second[i], 1)
        high_across = send(high_next[i, -1], second[i], -1)
        pieces.append(
            [
                (low[i], high[i]),
                (low_next[i, 1], high_next[i, 1]),
                (low_next[i, -1], high_next[i, -1]),
                (low_across, high_across),
            ]
        )
    return pieces


def left_sector(sector, z_at, y_at):
    z = lax.rem(sector // SIDE + OFFSETS[z_at], SIDE)
    y = lax.rem(lax.rem(sector, SIDE) + OFFSETS[y_at], SIDE)
    return z * SIDE + y


def fold(block):
    return jnp.sum(block.reshape(block.shape[0] // 8, 8, block.shape[1]), axis=0)


def dot(a, b):
    return jnp.dot(a, b, preferred_element_type=jnp.float32)


def pick_kernel(sector, terms, sizes, left, half_a, half_b, blocks, sems):
    me = sector[0]
    copies = [pltpu.make_async_copy(left.at[0, terms[k, me], 0], blocks.at[k], sems.at[k]) for k in range(4)]
    for copy in copies:
        copy.start()
    size = blocks.shape[-1]
    keep = lax.broadcasted_iota(jnp.int32, (size, size), 0) < sizes[0, 0, me]
    for k, copy in enumerate(copies):
        copy.wait()
        block = jnp.where(keep, blocks[k].astype(jnp.float32), 0.0).astype(jnp.bfloat16)
        (half_a, half_b)[k // 2][k % 2] = block


def inner_product(a, k, terms, sources, vector, right):
    return dot(vector[sources[k, a]], right[terms[k, a]]).astype(jnp.bfloat16)


def left_block(pieces, z_at, y_at, k):
    if k < 2:
        return pieces[2 * z_at + y_at // 2][y_at % 2, k]
    return pieces[len(pieces) // 2 + 2 * y_at + z_at // 2][z_at % 2, k - 2]


def row_image(a, z_at, y_at, ks, terms, sources, vector, right, pieces):
    inner = [inner_product(a, k, terms, sources, vector, right) for k in ks]
    blocks = [left_block(pieces, z_at, y_at, k) for k in ks]
    return dot(jnp.concatenate(blocks, axis=1), jnp.concatenate(inner, axis=0))


WHOLE = [(z_at, y_at) for z_at in range(3) for y_at in range(3)]
LATE = [(3, 0), (3, 1), (3, 2), (0, 3), (1, 3), (2, 3), (3, 3)]


def late_ks(z_at, y_at):
    return ((0, 1) if z_at == 3 else ()) + ((2, 3) if y_at == 3 else ())


LATE_INNER = [(at, k) for at in LATE for k in late_ks(*at)]


def spread(total):
    return jnp.broadcast_to(jnp.sum(total, keepdims=True), (1, 128))


def first_kernel(sector, terms, sources, sizes, wave, right, *refs):
    pieces, (masked, right_live, field, part, inner, sums), (image,) = refs[:12], refs[12:18], refs[18:]
    size = image.shape[-1]
    me = sector[0]
    rows = lax.broadcasted_iota(jnp.int32, (size, size), 0)
    col_keep = lax.broadcasted_iota(jnp.int32, (size, size), 1) < sizes[0, 1, me]
    zero = jnp.zeros((8, size), jnp.float32)

    def mask_right(t, carry):
        right_live[t] = jnp.where(col_keep, right[0, t, 0].astype(jnp.float32), 0.0).astype(jnp.bfloat16)
        return carry

    def mask_wave(c, ww):
        keep = (rows < sizes[0, 0, c]) & col_keep
        w = jnp.where(keep, wave[0, c, 0].astype(jnp.float32), 0.0)
        masked[c] = w.astype(jnp.bfloat16)
        return ww + fold(w * w)

    lax.fori_loop(0, right_live.shape[0], mask_right, 0)
    ww = lax.fori_loop(0, masked.shape[0], mask_wave, zero)

    some_ww, some_wy = zero, zero
    for i, (z_at, y_at) in enumerate(WHOLE):
        a = left_sector(me, z_at, y_at)
        y = row_image(a, z_at, y_at, (0, 1, 2, 3), terms, sources, masked, right_live, pieces)
        image[i] = y
        w = masked[a].astype(jnp.float32)
        some_ww += fold(w * w)
        some_wy += fold(w * y)
    for i, (z_at, y_at) in enumerate(LATE[:6]):
        a = left_sector(me, z_at, y_at)
        ks = (2, 3) if z_at == 3 else (0, 1)
        part[i] = row_image(a, z_at, y_at, ks, terms, sources, masked, right_live, pieces)
    for i, ((z_at, y_at), k) in enumerate(LATE_INNER):
        a = left_sector(me, z_at, y_at)
        inner[i] = inner_product(a, k, terms, sources, masked, right_live)

    some_ww = jnp.sum(some_ww, keepdims=True)
    some_wy = jnp.sum(some_wy, keepdims=True)
    slope = jnp.where(some_ww > 0.0, some_wy / jnp.where(some_ww > 0.0, some_ww, 1.0), 0.0)
    wu, uu = zero, zero
    for i, (z_at, y_at) in enumerate(WHOLE):
        a = left_sector(me, z_at, y_at)
        w = masked[a].astype(jnp.float32)
        u = (image[i] - slope * w).astype(jnp.bfloat16)
        field[i] = u
        u = u.astype(jnp.float32)
        wu += fold(w * u)
        uu += fold(u * u)
    slope = jnp.broadcast_to(slope, (1, 128))
    sums[...] = jnp.concatenate([spread(ww), spread(wu), spread(uu)] + [slope] * 5, axis=0)


def second_kernel(sector, terms, sources, masked, right_live, field_some, part, inner, sums_first, *refs):
    pieces, (field, image, sums) = refs[:16], refs[16:]
    size = image.shape[-1]
    me = sector[0]
    zero = jnp.zeros((8, size), jnp.float32)
    slope = sums_first[3:4, :1]
    wu, uu = zero, zero
    at = 0
    for i, (z_at, y_at) in enumerate(LATE):
        a = left_sector(me, z_at, y_at)
        ks = late_ks(z_at, y_at)
        blocks = [left_block(pieces, z_at, y_at, k) for k in ks]
        late_inner = jnp.concatenate([inner[at + j] for j in range(len(ks))], axis=0)
        at += len(ks)
        y = dot(jnp.concatenate(blocks, axis=1), late_inner)
        if i < 6:
            y += part[i]
        w = masked[a].astype(jnp.float32)
        u = (y - slope * w).astype(jnp.bfloat16)
        field[a] = u
        u = u.astype(jnp.float32)
        wu += fold(w * u)
        uu += fold(u * u)
    for i, (z_at, y_at) in enumerate(WHOLE):
        field[left_sector(me, z_at, y_at)] = field_some[i]

    wv, uv, vv = zero, zero, zero
    for z_at in range(4):
        for y_at in range(4):
            a = left_sector(me, z_at, y_at)
            v = row_image(a, z_at, y_at, (0, 1, 2, 3), terms, sources, field, right_live, pieces)
            image[a] = v
            wv += fold(masked[a].astype(jnp.float32) * v)
            uv += fold(field[a].astype(jnp.float32) * v)
            vv += fold(v * v)

    head = sums_first[...]
    block = jnp.concatenate(
        [
            head[0:1],
            head[1:2] + spread(wu),
            head[2:3] + spread(uu),
            spread(wv),
            spread(uv),
            spread(vv),
            head[3:4],
            head[3:4],
        ],
        axis=0,
    )
    sums[...] = jnp.broadcast_to(block[None], sums.shape)


def last_kernel(cells, gathered, own, masked, field, image, out, projected, weights):
    step = pl.program_id(0)

    @pl.when(step == 0)
    def _():
        g = gathered[...]
        ww, wu, uu, wv, uv, vv, slope = (g[:, j, :] for j in range(7))

        def total(values):
            return jnp.sum(values, axis=0, keepdims=True) / cells

        alpha = lax.rsqrt(total(ww) + epsilon)
        wy = wu + slope * ww
        uy = uu + slope * wu
        theta = alpha * alpha * total(wy)
        delta = theta - slope
        beta = lax.rsqrt(alpha * alpha * total(uu - 2.0 * delta * wu + delta * delta * ww) + epsilon)
        scale = alpha * beta
        upper = alpha * scale * total(wv - delta * wy)
        lower = scale * scale * total(uv - delta * uy - delta * (wv - delta * wy))
        cu = delta + lower
        cw = delta * slope - lower * delta + upper / beta
        squares = vv + cu * cu * uu + cw * cw * ww - 2.0 * (cu * uv + cw * wv - cu * cw * wu)
        gamma = lax.rsqrt(scale * scale * total(squares) + epsilon)
        factor = gamma * scale
        own_slope = own[0, 6:7, :]
        own_delta = theta - own_slope
        own_cu = own_delta + lower
        own_cw = own_delta * own_slope - lower * own_delta + upper / beta
        weights[...] = jnp.concatenate([factor, factor * own_cu, factor * own_cw], axis=0)
        lane = lax.broadcasted_iota(jnp.int32, theta.shape, 1)
        entries = jnp.where(lane == 0, theta, jnp.where(lane == 1, upper, lower))
        projected[...] = entries[:, :3]

    def wide(j):
        row = weights[j : j + 1, :]
        return jnp.concatenate([row] * (out.shape[-1] // 128), axis=1)[None]

    per_step = out.shape[1]
    here = pl.ds(step * per_step, per_step)
    out[0, :, 0] = (
        image[here] * wide(0)
        - field[here].astype(jnp.float32) * wide(1)
        - masked[here].astype(jnp.float32) * wide(2)
    )


def per_device(wavefunction, left_env, right_env, term_table, source_table, live_sizes):
    sectors, size = wavefunction.shape[1], wavefunction.shape[3]
    terms_count = left_env.shape[1]
    smem = pl.BlockSpec(memory_space=pltpu.SMEM)
    vmem = pl.BlockSpec(memory_space=pltpu.VMEM)
    bf16, f32 = jnp.bfloat16, jnp.float32
    sector = lax.axis_index("sector").astype(jnp.int32)[None]
    terms, sources = term_table.T, source_table.T

    def blocks(count, dtype):
        return jax.ShapeDtypeStruct((count, size, size), dtype)

    half_a, half_b = pl.pallas_call(
        pick_kernel,
        out_shape=(blocks(2, bf16), blocks(2, bf16)),
        in_specs=[smem, smem, smem, pl.BlockSpec(memory_space=pltpu.HBM)],
        out_specs=(vmem, vmem),
        scratch_shapes=[pltpu.VMEM((4, size, size), bf16), pltpu.SemaphoreType.DMA((4,))],
        compiler_params=pltpu.CompilerParams(vmem_limit_bytes=4 * MIB),
        name="pick_left",
    )(sector, terms, live_sizes, left_env)

    pairs_a, pairs_b = gather_halves(half_a, half_b)
    early = [p for pairs in (pairs_a, pairs_b) for pair in pairs[:3] for p in pair]
    every = [p for pairs in (pairs_a, pairs_b) for pair in pairs for p in pair]
    count = lax.axis_size("section")
    partner = lax.ppermute(
        right_env, "section", [(s, s ^ 1) for s in range(count)]
    )

    flop = 2 * size * size * size
    masked, right_live, field_some, part, inner, sums_first = pl.pallas_call(
        first_kernel,
        out_shape=(
            blocks(sectors, bf16),
            blocks(terms_count, bf16),
            blocks(len(WHOLE), bf16),
            blocks(6, f32),
            blocks(len(LATE_INNER), bf16),
            jax.ShapeDtypeStruct((8, 128), f32),
        ),
        in_specs=[smem] * 4 + [vmem] * 14,
        out_specs=(vmem,) * 6,
        scratch_shapes=[pltpu.VMEM((len(WHOLE), size, size), f32)],
        compiler_params=pltpu.CompilerParams(vmem_limit_bytes=20 * MIB),
        name="first_image",
    )(sector, terms, sources, live_sizes, wavefunction, partner, *early)

    field, image, sums = pl.pallas_call(
        second_kernel,
        out_shape=(
            blocks(sectors, bf16),
            blocks(sectors, f32),
            jax.ShapeDtypeStruct((sectors, 8, 128), f32),
        ),
        in_specs=[smem] * 3 + [vmem] * 22,
        out_specs=(vmem,) * 3,
        compiler_params=pltpu.CompilerParams(vmem_limit_bytes=20 * MIB),
        cost_estimate=pl.CostEstimate(flops=144 * flop, bytes_accessed=24 * MIB, transcendentals=0),
        name="second_image",
    )(sector, terms, sources, masked, right_live, field_some, part, inner, sums_first, *every)

    gathered = lax.all_to_all(sums, "sector", 0, 0)
    per_step = 2
    cells = float(sectors * sectors * size * size)
    next_basis, projected = pl.pallas_call(
        functools.partial(last_kernel, cells),
        grid=(sectors // per_step,),
        out_shape=(
            jax.ShapeDtypeStruct((1, sectors, 1, size, size), f32),
            jax.ShapeDtypeStruct((1, 3), f32),
        ),
        in_specs=[vmem] * 5,
        out_specs=(
            pl.BlockSpec((1, per_step, 1, size, size), lambda i: (0, i, 0, 0, 0)),
            pl.BlockSpec((1, 3), lambda i: (0, 0)),
        ),
        scratch_shapes=[pltpu.VMEM((3, 128), f32)],
        compiler_params=pltpu.CompilerParams(vmem_limit_bytes=8 * MIB),
        name="next_basis",
    )(gathered, sums, masked, field, image)
    return next_basis, projected


def solution(mesh):
    in_specs = (
        P("section", None, "sector", None, None),
        P("section", None, "sector", None, None),
        P("section", None, "sector", None, None),
        P(),
        P(),
        P("section", None, None),
    )
    out_specs = (P("section", None, "sector", None, None), P("section", None))
    return jax.shard_map(
        per_device, mesh=mesh, in_specs=in_specs, out_specs=out_specs, check_vma=False
    )
```

```python
import functools

import jax
import jax.numpy as jnp
from jax import lax
from jax.experimental import pallas as pl
from jax.experimental.pallas import tpu as pltpu
from jax.sharding import PartitionSpec as P

epsilon = 1e-06
SIDE = 4
OFFSETS = (0, 3, 1, 2)
MIB = 1 << 20


def ring(dz, dy):
    return [
        (z * SIDE + y, ((z + dz) % SIDE) * SIDE + (y + dy) % SIDE)
        for z in range(SIDE)
        for y in range(SIDE)
    ]


def along(axis, step):
    return ring(step % SIDE, 0) if axis == "z" else ring(0, step % SIDE)


def send(block, axis, step):
    return lax.ppermute(block, "sector", along(axis, step))


def after(value, *results):
    return lax.optimization_barrier((value, *results))[0]


def gather_halves(half_a, half_b, stage_a, stage_b):
    own, kept = (half_a, half_b), (stage_a, stage_b)
    first, second = ("y", "z"), ("z", "y")
    near = {(i, step): send(own[i], first[i], step) for i in range(2) for step in (1, -1)}
    across = [send(near[i, 1], first[i], 1) for i in range(2)]
    last = {(first[i], step): near[i, step] for i in range(2) for step in (1, -1)}
    last.update({(first[i], 1): across[i] for i in range(2)})
    low = [jnp.stack([kept[i], near[i, 1]]) for i in range(2)]
    high = [jnp.stack([near[i, -1], across[i]]) for i in range(2)]
    low_next, high_next = {}, {}
    for i in range(2):
        for step in (1, -1):
            low_next[i, step] = send(after(low[i], last[second[i], step]), second[i], step)
    for i in range(2):
        for step in (1, -1):
            high_next[i, step] = send(after(high[i], low_next[i, step]), second[i], step)
    pieces = []
    for i in range(2):
        one, two = low_next[i, 1], low_next[i, -1]
        up = jnp.concatenate([one[0, :1], one[1]])
        down = jnp.concatenate([high_next[i, -1].reshape(4, *two.shape[2:]), two[0, 1:]])
        pieces.append(
            [
                low[i],
                high[i],
                low_next[i, 1],
                high_next[i, 1],
                low_next[i, -1],
                high_next[i, -1],
                send(after(up, high_next[i, 1]), second[i], 1),
                send(down, second[i], -1),
            ]
        )
    return pieces


def left_sector(sector, z_at, y_at):
    z = lax.rem(sector // SIDE + OFFSETS[z_at], SIDE)
    y = lax.rem(lax.rem(sector, SIDE) + OFFSETS[y_at], SIDE)
    return z * SIDE + y


def fold(block):
    return jnp.sum(block.reshape(block.shape[0] // 8, 8, block.shape[1]), axis=0)


def dot(a, b):
    return jnp.dot(a, b, preferred_element_type=jnp.float32)


def pick_kernel(sector, terms, sizes, left, half_a, half_b, blocks, sems):
    me = sector[0]
    copies = [pltpu.make_async_copy(left.at[0, terms[k, me], 0], blocks.at[k], sems.at[k]) for k in range(4)]
    for copy in copies:
        copy.start()
    size = blocks.shape[-1]
    keep = lax.broadcasted_iota(jnp.int32, (size, size), 0) < sizes[0, 0, me]
    for k, copy in enumerate(copies):
        copy.wait()
        block = jnp.where(keep, blocks[k].astype(jnp.float32), 0.0).astype(jnp.bfloat16)
        (half_a, half_b)[k // 2][k % 2] = block


def stage_kernel(half_a, half_b, stage_a, stage_b):
    stage_a[...] = half_a[...]
    stage_b[...] = half_b[...]


def inner_product(a, k, terms, sources, vector, right):
    return dot(vector[sources[k, a]], right[terms[k, a]]).astype(jnp.bfloat16)


ACROSS = (((6, 0), (7, 4)), ((6, 1), (6, 2)), ((7, 0), (7, 1)), ((7, 2), (7, 3)))


def left_block(pieces, z_at, y_at, k):
    half = k // 2
    first_at, second_at = ((y_at, z_at), (z_at, y_at))[half]
    of_half = pieces[len(pieces) // 2 * half :]
    if second_at == 3:
        array, entry = ACROSS[first_at][k % 2]
        return of_half[array][entry]
    return of_half[2 * second_at + first_at // 2][first_at % 2, k % 2]


def row_image(a, z_at, y_at, ks, terms, sources, vector, right, pieces):
    inner = [inner_product(a, k, terms, sources, vector, right) for k in ks]
    blocks = [left_block(pieces, z_at, y_at, k) for k in ks]
    return dot(jnp.concatenate(blocks, axis=1), jnp.concatenate(inner, axis=0))


WHOLE = [(z_at, y_at) for z_at in range(3) for y_at in range(3)]
LATE = [(3, 0), (3, 1), (3, 2), (0, 3), (1, 3), (2, 3), (3, 3)]


def late_ks(z_at, y_at):
    return ((0, 1) if z_at == 3 else ()) + ((2, 3) if y_at == 3 else ())


LATE_INNER = [(at, k) for at in LATE for k in late_ks(*at)]


def spread(total):
    return jnp.broadcast_to(jnp.sum(total, keepdims=True), (1, 128))


def first_kernel(sector, terms, sources, sizes, wave, right, *refs):
    pieces, (masked, right_live, field, part, inner, sums), (image,) = refs[:12], refs[12:18], refs[18:]
    size = image.shape[-1]
    me = sector[0]
    rows = lax.broadcasted_iota(jnp.int32, (size, size), 0)
    col_keep = lax.broadcasted_iota(jnp.int32, (size, size), 1) < sizes[0, 1, me]
    zero = jnp.zeros((8, size), jnp.float32)

    def mask_right(t, carry):
        right_live[t] = jnp.where(col_keep, right[0, t, 0].astype(jnp.float32), 0.0).astype(jnp.bfloat16)
        return carry

    def mask_wave(c, ww):
        keep = (rows < sizes[0, 0, c]) & col_keep
        w = jnp.where(keep, wave[0, c, 0].astype(jnp.float32), 0.0)
        masked[c] = w.astype(jnp.bfloat16)
        return ww + fold(w * w)

    lax.fori_loop(0, right_live.shape[0], mask_right, 0)
    ww = lax.fori_loop(0, masked.shape[0], mask_wave, zero)

    some_ww, some_wy = zero, zero
    for i, (z_at, y_at) in enumerate(WHOLE):
        a = left_sector(me, z_at, y_at)
        y = row_image(a, z_at, y_at, (0, 1, 2, 3), terms, sources, masked, right_live, pieces)
        image[i] = y
        w = masked[a].astype(jnp.float32)
        some_ww += fold(w * w)
        some_wy += fold(w * y)
    for i, (z_at, y_at) in enumerate(LATE[:6]):
        a = left_sector(me, z_at, y_at)
        ks = (2, 3) if z_at == 3 else (0, 1)
        part[i] = row_image(a, z_at, y_at, ks, terms, sources, masked, right_live, pieces)
    for i, ((z_at, y_at), k) in enumerate(LATE_INNER):
        a = left_sector(me, z_at, y_at)
        inner[i] = inner_product(a, k, terms, sources, masked, right_live)

    some_ww = jnp.sum(some_ww, keepdims=True)
    some_wy = jnp.sum(some_wy, keepdims=True)
    slope = jnp.where(some_ww > 0.0, some_wy / jnp.where(some_ww > 0.0, some_ww, 1.0), 0.0)
    wu, uu = zero, zero
    for i, (z_at, y_at) in enumerate(WHOLE):
        a = left_sector(me, z_at, y_at)
        w = masked[a].astype(jnp.float32)
        u = (image[i] - slope * w).astype(jnp.bfloat16)
        field[i] = u
        u = u.astype(jnp.float32)
        wu += fold(w * u)
        uu += fold(u * u)
    slope = jnp.broadcast_to(slope, (1, 128))
    sums[...] = jnp.concatenate([spread(ww), spread(wu), spread(uu)] + [slope] * 5, axis=0)


def second_kernel(sector, terms, sources, masked, right_live, field_some, part, inner, sums_first, *refs):
    pieces, (field, image, sums) = refs[:16], refs[16:]
    size = image.shape[-1]
    me = sector[0]
    zero = jnp.zeros((8, size), jnp.float32)
    slope = sums_first[3:4, :1]
    wu, uu = zero, zero
    at = 0
    for i, (z_at, y_at) in enumerate(LATE):
        a = left_sector(me, z_at, y_at)
        ks = late_ks(z_at, y_at)
        blocks = [left_block(pieces, z_at, y_at, k) for k in ks]
        late_inner = jnp.concatenate([inner[at + j] for j in range(len(ks))], axis=0)
        at += len(ks)
        y = dot(jnp.concatenate(blocks, axis=1), late_inner)
        if i < 6:
            y += part[i]
        w = masked[a].astype(jnp.float32)
        u = (y - slope * w).astype(jnp.bfloat16)
        field[a] = u
        u = u.astype(jnp.float32)
        wu += fold(w * u)
        uu += fold(u * u)
    for i, (z_at, y_at) in enumerate(WHOLE):
        field[left_sector(me, z_at, y_at)] = field_some[i]

    wv, uv, vv = zero, zero, zero
    for z_at in range(4):
        for y_at in range(4):
            a = left_sector(me, z_at, y_at)
            v = row_image(a, z_at, y_at, (0, 1, 2, 3), terms, sources, field, right_live, pieces)
            image[a] = v
            wv += fold(masked[a].astype(jnp.float32) * v)
            uv += fold(field[a].astype(jnp.float32) * v)
            vv += fold(v * v)

    head = sums_first[...]
    block = jnp.concatenate(
        [
            head[0:1],
            head[1:2] + spread(wu),
            head[2:3] + spread(uu),
            spread(wv),
            spread(uv),
            spread(vv),
            head[3:4],
            head[3:4],
        ],
        axis=0,
    )
    sums[...] = jnp.broadcast_to(block[None], sums.shape)


def last_kernel(cells, gathered, own, masked, field, image, out, projected, weights):
    step = pl.program_id(0)

    @pl.when(step == 0)
    def _():
        g = gathered[...]
        ww, wu, uu, wv, uv, vv, slope = (g[:, j, :] for j in range(7))

        def total(values):
            return jnp.sum(values, axis=0, keepdims=True) / cells

        alpha = lax.rsqrt(total(ww) + epsilon)
        wy = wu + slope * ww
        uy = uu + slope * wu
        theta = alpha * alpha * total(wy)
        delta = theta - slope
        beta = lax.rsqrt(alpha * alpha * total(uu - 2.0 * delta * wu + delta * delta * ww) + epsilon)
        scale = alpha * beta
        upper = alpha * scale * total(wv - delta * wy)
        lower = scale * scale * total(uv - delta * uy - delta * (wv - delta * wy))
        cu = delta + lower
        cw = delta * slope - lower * delta + upper / beta
        squares = vv + cu * cu * uu + cw * cw * ww - 2.0 * (cu * uv + cw * wv - cu * cw * wu)
        gamma = lax.rsqrt(scale * scale * total(squares) + epsilon)
        factor = gamma * scale
        own_slope = own[0, 6:7, :]
        own_delta = theta - own_slope
        own_cu = own_delta + lower
        own_cw = own_delta * own_slope - lower * own_delta + upper / beta
        weights[...] = jnp.concatenate([factor, factor * own_cu, factor * own_cw], axis=0)
        lane = lax.broadcasted_iota(jnp.int32, theta.shape, 1)
        entries = jnp.where(lane == 0, theta, jnp.where(lane == 1, upper, lower))
        projected[...] = entries[:, :3]

    def wide(j):
        row = weights[j : j + 1, :]
        return jnp.concatenate([row] * (out.shape[-1] // 128), axis=1)[None]

    per_step = out.shape[1]
    here = pl.ds(step * per_step, per_step)
    out[0, :, 0] = (
        image[here] * wide(0)
        - field[here].astype(jnp.float32) * wide(1)
        - masked[here].astype(jnp.float32) * wide(2)
    )


def per_device(wavefunction, left_env, right_env, term_table, source_table, live_sizes):
    sectors, size = wavefunction.shape[1], wavefunction.shape[3]
    terms_count = left_env.shape[1]
    smem = pl.BlockSpec(memory_space=pltpu.SMEM)
    vmem = pl.BlockSpec(memory_space=pltpu.VMEM)
    bf16, f32 = jnp.bfloat16, jnp.float32
    sector = lax.axis_index("sector").astype(jnp.int32)[None]
    terms, sources = term_table.T, source_table.T

    def blocks(count, dtype):
        return jax.ShapeDtypeStruct((count, size, size), dtype)

    half_a, half_b = pl.pallas_call(
        pick_kernel,
        out_shape=(blocks(2, bf16), blocks(2, bf16)),
        in_specs=[smem, smem, smem, pl.BlockSpec(memory_space=pltpu.HBM)],
        out_specs=(vmem, vmem),
        scratch_shapes=[pltpu.VMEM((4, size, size), bf16), pltpu.SemaphoreType.DMA((4,))],
        compiler_params=pltpu.CompilerParams(vmem_limit_bytes=60 * MIB),
        name="pick_left",
    )(sector, terms, live_sizes, left_env)

    stage_a, stage_b = pl.pallas_call(
        stage_kernel,
        out_shape=(blocks(2, bf16), blocks(2, bf16)),
        in_specs=[vmem, vmem],
        out_specs=(vmem, vmem),
        compiler_params=pltpu.CompilerParams(vmem_limit_bytes=4 * MIB),
        cost_estimate=pl.CostEstimate(flops=1 << 20, bytes_accessed=MIB, transcendentals=0),
        name="stage",
    )(half_a, half_b)
    pieces_a, pieces_b = gather_halves(half_a, half_b, stage_a, stage_b)
    early = pieces_a[:6] + pieces_b[:6]
    every = pieces_a + pieces_b
    count = lax.axis_size("section")
    partner = lax.ppermute(
        right_env, "section", [(s, s ^ 1) for s in range(count)]
    )

    flop = 2 * size * size * size
    masked, right_live, field_some, part, inner, sums_first = pl.pallas_call(
        first_kernel,
        out_shape=(
            blocks(sectors, bf16),
            blocks(terms_count, bf16),
            blocks(len(WHOLE), bf16),
            blocks(6, f32),
            blocks(len(LATE_INNER), bf16),
            jax.ShapeDtypeStruct((8, 128), f32),
        ),
        in_specs=[smem] * 4 + [vmem] * 14,
        out_specs=(vmem,) * 6,
        scratch_shapes=[pltpu.VMEM((len(WHOLE), size, size), f32)],
        compiler_params=pltpu.CompilerParams(vmem_limit_bytes=20 * MIB),
        name="first_image",
    )(sector, terms, sources, live_sizes, wavefunction, partner, *early)

    field, image, sums = pl.pallas_call(
        second_kernel,
        out_shape=(
            blocks(sectors, bf16),
            blocks(sectors, f32),
            jax.ShapeDtypeStruct((sectors, 8, 128), f32),
        ),
        in_specs=[smem] * 3 + [vmem] * 22,
        out_specs=(vmem,) * 3,
        compiler_params=pltpu.CompilerParams(vmem_limit_bytes=20 * MIB),
        cost_estimate=pl.CostEstimate(flops=144 * flop, bytes_accessed=24 * MIB, transcendentals=0),
        name="second_image",
    )(sector, terms, sources, masked, right_live, field_some, part, inner, sums_first, *every)

    gathered = lax.all_to_all(sums, "sector", 0, 0)
    per_step = 8
    cells = float(sectors * sectors * size * size)
    next_basis, projected = pl.pallas_call(
        functools.partial(last_kernel, cells),
        grid=(sectors // per_step,),
        out_shape=(
            jax.ShapeDtypeStruct((1, sectors, 1, size, size), f32),
            jax.ShapeDtypeStruct((1, 3), f32),
        ),
        in_specs=[vmem] * 5,
        out_specs=(
            pl.BlockSpec((1, per_step, 1, size, size), lambda i: (0, i, 0, 0, 0)),
            pl.BlockSpec((1, 3), lambda i: (0, 0)),
        ),
        scratch_shapes=[pltpu.VMEM((3, 128), f32)],
        compiler_params=pltpu.CompilerParams(vmem_limit_bytes=12 * MIB),
        name="next_basis",
    )(gathered, sums, masked, field, image)
    return next_basis, projected


def solution(mesh):
    in_specs = (
        P("section", None, "sector", None, None),
        P("section", None, "sector", None, None),
        P("section", None, "sector", None, None),
        P(),
        P(),
        P("section", None, None),
    )
    out_specs = (P("section", None, "sector", None, None), P("section", None))
    return jax.shard_map(
        per_device, mesh=mesh, in_specs=in_specs, out_specs=out_specs, check_vma=False
    )
```

```python
import functools

import jax
import jax.numpy as jnp
from jax import lax
from jax.experimental import pallas as pl
from jax.experimental.pallas import tpu as pltpu
from jax.sharding import PartitionSpec as P

epsilon = 1e-06
SIDE = 4
OFFSETS = (0, 3, 1, 2)
MIB = 1 << 20


def ring(dz, dy):
    return [
        (z * SIDE + y, ((z + dz) % SIDE) * SIDE + (y + dy) % SIDE)
        for z in range(SIDE)
        for y in range(SIDE)
    ]


def along(axis, step):
    return ring(step % SIDE, 0) if axis == "z" else ring(0, step % SIDE)


def send(block, axis, step):
    return lax.ppermute(block, "sector", along(axis, step))


def after(value, *results):
    return lax.optimization_barrier((value, *results))[0]


def gather_halves(half_a, half_b, stage_a, stage_b, gate):
    own, kept = (half_a, half_b), (stage_a, stage_b)
    first, second = ("y", "z"), ("z", "y")
    near = {(i, step): send(own[i], first[i], step) for i in range(2) for step in (1, -1)}
    across = [send(near[i, 1], first[i], 1) for i in range(2)]
    last = {(first[i], step): near[i, step] for i in range(2) for step in (1, -1)}
    last.update({(first[i], 1): across[i] for i in range(2)})
    low = [jnp.stack([kept[i], near[i, 1]]) for i in range(2)]
    high = [jnp.stack([near[i, -1], across[i]]) for i in range(2)]
    low_next, high_next = {}, {}
    for i in range(2):
        for step in (1, -1):
            low_next[i, step] = send(after(low[i], last[second[i], step]), second[i], step)
    for i in range(2):
        for step in (1, -1):
            high_next[i, step] = send(after(high[i], low_next[i, step]), second[i], step)
    pieces = []
    for i in range(2):
        one, two = low_next[i, 1], low_next[i, -1]
        up = jnp.concatenate([one[0, :1], one[1]])
        down = jnp.concatenate([high_next[i, -1].reshape(4, *two.shape[2:]), two[0, 1:]])
        pieces.append(
            [
                low[i],
                high[i],
                low_next[i, 1],
                high_next[i, 1],
                low_next[i, -1],
                high_next[i, -1],
                send(after(up, high_next[i, 1], gate), second[i], 1),
                send(down, second[i], -1),
            ]
        )
    return pieces


def left_sector(sector, z_at, y_at):
    z = lax.rem(sector // SIDE + OFFSETS[z_at], SIDE)
    y = lax.rem(lax.rem(sector, SIDE) + OFFSETS[y_at], SIDE)
    return z * SIDE + y


def fold(block):
    return jnp.sum(block.reshape(block.shape[0] // 8, 8, block.shape[1]), axis=0)


def dot(a, b):
    return jnp.dot(a, b, preferred_element_type=jnp.float32)


def pick_kernel(sector, terms, sizes, left, half_a, half_b, blocks, sems):
    me = sector[0]
    copies = [pltpu.make_async_copy(left.at[0, terms[k, me], 0], blocks.at[k], sems.at[k]) for k in range(4)]
    for copy in copies:
        copy.start()
    size = blocks.shape[-1]
    keep = lax.broadcasted_iota(jnp.int32, (size, size), 0) < sizes[0, 0, me]
    for k, copy in enumerate(copies):
        copy.wait()
        block = jnp.where(keep, blocks[k].astype(jnp.float32), 0.0).astype(jnp.bfloat16)
        (half_a, half_b)[k // 2][k % 2] = block


def stage_kernel(half_a, half_b, stage_a, stage_b):
    stage_a[...] = half_a[...]
    stage_b[...] = half_b[...]


def inner_product(a, k, terms, sources, vector, right):
    return dot(vector[sources[k, a]], right[terms[k, a]]).astype(jnp.bfloat16)


ACROSS = (((6, 0), (7, 4)), ((6, 1), (6, 2)), ((7, 0), (7, 1)), ((7, 2), (7, 3)))


def left_block(pieces, z_at, y_at, k):
    half = k // 2
    first_at, second_at = ((y_at, z_at), (z_at, y_at))[half]
    of_half = pieces[len(pieces) // 2 * half :]
    if second_at == 3:
        array, entry = ACROSS[first_at][k % 2]
        return of_half[array][entry]
    return of_half[2 * second_at + first_at // 2][first_at % 2, k % 2]


def left_row(pieces, z_at, y_at, ks):
    return jnp.concatenate([left_block(pieces, z_at, y_at, k) for k in ks], axis=1)


def row_image(a, z_at, y_at, terms, sources, vector, right, pieces):
    inner = [inner_product(a, k, terms, sources, vector, right) for k in range(4)]
    return dot(left_row(pieces, z_at, y_at, range(4)), jnp.concatenate(inner, axis=0))


def inner_rows(inner, z_at, y_at, ks):
    at = 4 * (4 * z_at + y_at) + ks[0]
    return inner[at : at + len(ks)].reshape(len(ks) * inner.shape[1], inner.shape[2])


WHOLE = [(z_at, y_at) for z_at in range(3) for y_at in range(3)]
LATE = [(3, 0), (3, 1), (3, 2), (0, 3), (1, 3), (2, 3), (3, 3)]


def late_ks(z_at, y_at):
    return ((0, 1) if z_at == 3 else ()) + ((2, 3) if y_at == 3 else ())


def spread(total):
    return jnp.broadcast_to(jnp.sum(total, keepdims=True), (1, 128))


def inner_kernel(sector, terms, sources, sizes, wave, right, masked, right_live, inner, sums):
    size = inner.shape[-1]
    me = sector[0]
    rows = lax.broadcasted_iota(jnp.int32, (size, size), 0)
    col_keep = lax.broadcasted_iota(jnp.int32, (size, size), 1) < sizes[0, 1, me]

    def mask_right(t, carry):
        right_live[t] = jnp.where(col_keep, right[0, t, 0].astype(jnp.float32), 0.0).astype(jnp.bfloat16)
        return carry

    def mask_wave(c, ww):
        keep = (rows < sizes[0, 0, c]) & col_keep
        w = jnp.where(keep, wave[0, c, 0].astype(jnp.float32), 0.0)
        masked[c] = w.astype(jnp.bfloat16)
        return ww + fold(w * w)

    lax.fori_loop(0, right_live.shape[0], mask_right, 0)
    ww = lax.fori_loop(0, masked.shape[0], mask_wave, jnp.zeros((8, size), jnp.float32))
    for z_at in range(4):
        for y_at in range(4):
            a = left_sector(me, z_at, y_at)
            for k in range(4):
                inner[4 * (4 * z_at + y_at) + k] = inner_product(a, k, terms, sources, masked, right_live)
    sums[...] = jnp.broadcast_to(spread(ww), sums.shape)


def first_kernel(sector, masked, inner, sums_wave, *refs):
    pieces, (field, part, sums), (image,) = refs[:12], refs[12:15], refs[15:]
    size = image.shape[-1]
    me = sector[0]
    zero = jnp.zeros((8, size), jnp.float32)
    some_ww, some_wy = zero, zero
    for i, (z_at, y_at) in enumerate(WHOLE):
        ks = (0, 1, 2, 3)
        y = dot(left_row(pieces, z_at, y_at, ks), inner_rows(inner, z_at, y_at, ks))
        image[i] = y
        w = masked[left_sector(me, z_at, y_at)].astype(jnp.float32)
        some_ww += fold(w * w)
        some_wy += fold(w * y)
    for i, (z_at, y_at) in enumerate(LATE[:6]):
        ks = (2, 3) if z_at == 3 else (0, 1)
        part[i] = dot(left_row(pieces, z_at, y_at, ks), inner_rows(inner, z_at, y_at, ks))

    some_ww = jnp.sum(some_ww, keepdims=True)
    some_wy = jnp.sum(some_wy, keepdims=True)
    slope = jnp.where(some_ww > 0.0, some_wy / jnp.where(some_ww > 0.0, some_ww, 1.0), 0.0)
    wu, uu = zero, zero
    for i, (z_at, y_at) in enumerate(WHOLE):
        w = masked[left_sector(me, z_at, y_at)].astype(jnp.float32)
        u = (image[i] - slope * w).astype(jnp.bfloat16)
        field[i] = u
        u = u.astype(jnp.float32)
        wu += fold(w * u)
        uu += fold(u * u)
    slope = jnp.broadcast_to(slope, (1, 128))
    sums[...] = jnp.concatenate([sums_wave[0:1], spread(wu), spread(uu)] + [slope] * 5, axis=0)


def second_kernel(sector, terms, sources, masked, right_live, field_some, part, inner, sums_first, *refs):
    pieces, (field, image, sums) = refs[:16], refs[16:]
    size = image.shape[-1]
    me = sector[0]
    zero = jnp.zeros((8, size), jnp.float32)
    slope = sums_first[3:4, :1]
    wu, uu = zero, zero
    for i, (z_at, y_at) in enumerate(LATE):
        a = left_sector(me, z_at, y_at)
        ks = late_ks(z_at, y_at)
        y = dot(left_row(pieces, z_at, y_at, ks), inner_rows(inner, z_at, y_at, ks))
        if i < 6:
            y += part[i]
        w = masked[a].astype(jnp.float32)
        u = (y - slope * w).astype(jnp.bfloat16)
        field[a] = u
        u = u.astype(jnp.float32)
        wu += fold(w * u)
        uu += fold(u * u)
    for i, (z_at, y_at) in enumerate(WHOLE):
        field[left_sector(me, z_at, y_at)] = field_some[i]

    wv, uv, vv = zero, zero, zero
    for z_at in range(4):
        for y_at in range(4):
            a = left_sector(me, z_at, y_at)
            v = row_image(a, z_at, y_at, terms, sources, field, right_live, pieces)
            image[a] = v
            wv += fold(masked[a].astype(jnp.float32) * v)
            uv += fold(field[a].astype(jnp.float32) * v)
            vv += fold(v * v)

    head = sums_first[...]
    block = jnp.concatenate(
        [
            head[0:1],
            head[1:2] + spread(wu),
            head[2:3] + spread(uu),
            spread(wv),
            spread(uv),
            spread(vv),
            head[3:4],
            head[3:4],
        ],
        axis=0,
    )
    sums[...] = jnp.broadcast_to(block[None], sums.shape)


def last_kernel(cells, gathered, own, masked, field, image, out, projected, weights):
    step = pl.program_id(0)

    @pl.when(step == 0)
    def _():
        g = gathered[...]
        ww, wu, uu, wv, uv, vv, slope = (g[:, j, :] for j in range(7))

        def total(values):
            return jnp.sum(values, axis=0, keepdims=True) / cells

        alpha = lax.rsqrt(total(ww) + epsilon)
        wy = wu + slope * ww
        uy = uu + slope * wu
        theta = alpha * alpha * total(wy)
        delta = theta - slope
        beta = lax.rsqrt(alpha * alpha * total(uu - 2.0 * delta * wu + delta * delta * ww) + epsilon)
        scale = alpha * beta
        upper = alpha * scale * total(wv - delta * wy)
        lower = scale * scale * total(uv - delta * uy - delta * (wv - delta * wy))
        cu = delta + lower
        cw = delta * slope - lower * delta + upper / beta
        squares = vv + cu * cu * uu + cw * cw * ww - 2.0 * (cu * uv + cw * wv - cu * cw * wu)
        gamma = lax.rsqrt(scale * scale * total(squares) + epsilon)
        factor = gamma * scale
        own_slope = own[0, 6:7, :]
        own_delta = theta - own_slope
        own_cu = own_delta + lower
        own_cw = own_delta * own_slope - lower * own_delta + upper / beta
        weights[...] = jnp.concatenate([factor, factor * own_cu, factor * own_cw], axis=0)
        lane = lax.broadcasted_iota(jnp.int32, theta.shape, 1)
        entries = jnp.where(lane == 0, theta, jnp.where(lane == 1, upper, lower))
        projected[...] = entries[:, :3]

    def wide(j):
        row = weights[j : j + 1, :]
        return jnp.concatenate([row] * (out.shape[-1] // 128), axis=1)[None]

    per_step = out.shape[1]
    here = pl.ds(step * per_step, per_step)
    out[0, :, 0] = (
        image[here] * wide(0)
        - field[here].astype(jnp.float32) * wide(1)
        - masked[here].astype(jnp.float32) * wide(2)
    )


def per_device(wavefunction, left_env, right_env, term_table, source_table, live_sizes):
    sectors, size = wavefunction.shape[1], wavefunction.shape[3]
    terms_count = left_env.shape[1]
    smem = pl.BlockSpec(memory_space=pltpu.SMEM)
    vmem = pl.BlockSpec(memory_space=pltpu.VMEM)
    bf16, f32 = jnp.bfloat16, jnp.float32
    sector = lax.axis_index("sector").astype(jnp.int32)[None]
    terms, sources = term_table.T, source_table.T

    def blocks(count, dtype):
        return jax.ShapeDtypeStruct((count, size, size), dtype)

    half_a, half_b = pl.pallas_call(
        pick_kernel,
        out_shape=(blocks(2, bf16), blocks(2, bf16)),
        in_specs=[smem, smem, smem, pl.BlockSpec(memory_space=pltpu.HBM)],
        out_specs=(vmem, vmem),
        scratch_shapes=[pltpu.VMEM((4, size, size), bf16), pltpu.SemaphoreType.DMA((4,))],
        compiler_params=pltpu.CompilerParams(vmem_limit_bytes=60 * MIB),
        name="pick_left",
    )(sector, terms, live_sizes, left_env)

    stage_a, stage_b = pl.pallas_call(
        stage_kernel,
        out_shape=(blocks(2, bf16), blocks(2, bf16)),
        in_specs=[vmem, vmem],
        out_specs=(vmem, vmem),
        compiler_params=pltpu.CompilerParams(vmem_limit_bytes=4 * MIB),
        cost_estimate=pl.CostEstimate(flops=1 << 20, bytes_accessed=MIB, transcendentals=0),
        name="stage",
    )(half_a, half_b)
    count = lax.axis_size("section")
    partner = lax.ppermute(
        right_env, "section", [(s, s ^ 1) for s in range(count)]
    )

    flop = 2 * size * size * size
    row = jax.ShapeDtypeStruct((8, 128), f32)
    masked, right_live, inner, sums_wave = pl.pallas_call(
        inner_kernel,
        out_shape=(blocks(sectors, bf16), blocks(terms_count, bf16), blocks(4 * sectors, bf16), row),
        in_specs=[smem] * 4 + [vmem] * 2,
        out_specs=(vmem,) * 4,
        compiler_params=pltpu.CompilerParams(vmem_limit_bytes=16 * MIB),
        cost_estimate=pl.CostEstimate(flops=64 * flop, bytes_accessed=12 * MIB, transcendentals=0),
        name="inner_products",
    )(sector, terms, sources, live_sizes, wavefunction, partner)

    pieces_a, pieces_b = gather_halves(half_a, half_b, stage_a, stage_b, sums_wave)
    early = pieces_a[:6] + pieces_b[:6]
    every = pieces_a + pieces_b
    field_some, part, sums_first = pl.pallas_call(
        first_kernel,
        out_shape=(blocks(len(WHOLE), bf16), blocks(6, f32), row),
        in_specs=[smem] + [vmem] * 15,
        out_specs=(vmem,) * 3,
        scratch_shapes=[pltpu.VMEM((len(WHOLE), size, size), f32)],
        compiler_params=pltpu.CompilerParams(vmem_limit_bytes=12 * MIB),
        name="first_image",
    )(sector, masked, inner, sums_wave, *early)

    field, image, sums = pl.pallas_call(
        second_kernel,
        out_shape=(
            blocks(sectors, bf16),
            blocks(sectors, f32),
            jax.ShapeDtypeStruct((sectors, 8, 128), f32),
        ),
        in_specs=[smem] * 3 + [vmem] * 22,
        out_specs=(vmem,) * 3,
        compiler_params=pltpu.CompilerParams(vmem_limit_bytes=20 * MIB),
        cost_estimate=pl.CostEstimate(flops=144 * flop, bytes_accessed=24 * MIB, transcendentals=0),
        name="second_image",
    )(sector, terms, sources, masked, right_live, field_some, part, inner, sums_first, *every)

    gathered = lax.all_to_all(sums, "sector", 0, 0)
    per_step = 8
    cells = float(sectors * sectors * size * size)
    next_basis, projected = pl.pallas_call(
        functools.partial(last_kernel, cells),
        grid=(sectors // per_step,),
        out_shape=(
            jax.ShapeDtypeStruct((1, sectors, 1, size, size), f32),
            jax.ShapeDtypeStruct((1, 3), f32),
        ),
        in_specs=[vmem] * 5,
        out_specs=(
            pl.BlockSpec((1, per_step, 1, size, size), lambda i: (0, i, 0, 0, 0)),
            pl.BlockSpec((1, 3), lambda i: (0, 0)),
        ),
        scratch_shapes=[pltpu.VMEM((3, 128), f32)],
        compiler_params=pltpu.CompilerParams(vmem_limit_bytes=12 * MIB),
        name="next_basis",
    )(gathered, sums, masked, field, image)
    return next_basis, projected


def solution(mesh):
    in_specs = (
        P("section", None, "sector", None, None),
        P("section", None, "sector", None, None),
        P("section", None, "sector", None, None),
        P(),
        P(),
        P("section", None, None),
    )
    out_specs = (P("section", None, "sector", None, None), P("section", None))
    return jax.shard_map(
        per_device, mesh=mesh, in_specs=in_specs, out_specs=out_specs, check_vma=False
    )
```

```python
import functools

import jax
import jax.numpy as jnp
from jax import lax
from jax.experimental import pallas as pl
from jax.experimental.pallas import tpu as pltpu
from jax.sharding import PartitionSpec as P

epsilon = 1e-06
SIDE = 4
OFFSETS = (0, 3, 1, 2)
MIB = 1 << 20


def ring(dz, dy):
    return [
        (z * SIDE + y, ((z + dz) % SIDE) * SIDE + (y + dy) % SIDE)
        for z in range(SIDE)
        for y in range(SIDE)
    ]


def along(axis, step):
    return ring(step % SIDE, 0) if axis == "z" else ring(0, step % SIDE)


def send(block, axis, step):
    return lax.ppermute(block, "sector", along(axis, step))


def after(value, *results):
    return lax.optimization_barrier((value, *results))[0]


def gather_halves(half_a, half_b, stage_a, stage_b, gate):
    own, kept = (half_a, half_b), (stage_a, stage_b)
    first, second = ("y", "z"), ("z", "y")
    near = {(i, step): send(own[i], first[i], step) for i in range(2) for step in (1, -1)}
    across = [send(near[i, 1], first[i], 1) for i in range(2)]
    last = {(first[i], step): near[i, step] for i in range(2) for step in (1, -1)}
    last.update({(first[i], 1): across[i] for i in range(2)})
    low = [jnp.stack([kept[i], near[i, 1]]) for i in range(2)]
    high = [jnp.stack([near[i, -1], across[i]]) for i in range(2)]
    low_next, high_next = {}, {}
    for i in range(2):
        for step in (1, -1):
            low_next[i, step] = send(after(low[i], last[second[i], step]), second[i], step)
    for i in range(2):
        for step in (1, -1):
            high_next[i, step] = send(after(high[i], low_next[i, step]), second[i], step)
    pieces = []
    for i in range(2):
        one, two = low_next[i, 1], low_next[i, -1]
        up = one[1]
        down = jnp.concatenate([high_next[i, -1].reshape(4, *two.shape[2:]), two[0]])
        pieces.append(
            [
                low[i],
                high[i],
                low_next[i, 1],
                high_next[i, 1],
                low_next[i, -1],
                high_next[i, -1],
                send(after(up, high_next[i, 1], gate), second[i], 1),
                send(down, second[i], -1),
            ]
        )
    return pieces


def left_sector(sector, z_at, y_at):
    z = lax.rem(sector // SIDE + OFFSETS[z_at], SIDE)
    y = lax.rem(lax.rem(sector, SIDE) + OFFSETS[y_at], SIDE)
    return z * SIDE + y


def fold(block):
    return jnp.sum(block.reshape(block.shape[0] // 8, 8, block.shape[1]), axis=0)


def dot(a, b):
    return jnp.dot(a, b, preferred_element_type=jnp.float32)


def pick_kernel(sector, terms, sizes, left, half_a, half_b, blocks, sems):
    me = sector[0]
    copies = [pltpu.make_async_copy(left.at[0, terms[k, me], 0], blocks.at[k], sems.at[k]) for k in range(4)]
    for copy in copies:
        copy.start()
    size = blocks.shape[-1]
    keep = lax.broadcasted_iota(jnp.int32, (size, size), 0) < sizes[0, 0, me]
    for k, copy in enumerate(copies):
        copy.wait()
        block = jnp.where(keep, blocks[k].astype(jnp.float32), 0.0).astype(jnp.bfloat16)
        (half_a, half_b)[k // 2][k % 2] = block


def stage_kernel(half_a, half_b, stage_a, stage_b):
    stage_a[...] = half_a[...]
    stage_b[...] = half_b[...]


def inner_product(a, k, terms, sources, vector, right):
    return dot(vector[sources[k, a]], right[terms[k, a]]).astype(jnp.bfloat16)


ACROSS = (((7, 4), (7, 5)), ((6, 0), (6, 1)), ((7, 0), (7, 1)), ((7, 2), (7, 3)))


def left_block(pieces, z_at, y_at, k):
    half = k // 2
    first_at, second_at = ((y_at, z_at), (z_at, y_at))[half]
    of_half = pieces[len(pieces) // 2 * half :]
    if second_at == 3:
        array, entry = ACROSS[first_at][k % 2]
        return of_half[array][entry]
    return of_half[2 * second_at + first_at // 2][first_at % 2, k % 2]


def left_row(pieces, z_at, y_at, ks):
    return jnp.concatenate([left_block(pieces, z_at, y_at, k) for k in ks], axis=1)


def row_image(a, z_at, y_at, terms, sources, vector, right, pieces):
    inner = [inner_product(a, k, terms, sources, vector, right) for k in range(4)]
    return dot(left_row(pieces, z_at, y_at, range(4)), jnp.concatenate(inner, axis=0))


def inner_rows(inner, z_at, y_at, ks):
    at = 4 * (4 * z_at + y_at) + ks[0]
    return inner[at : at + len(ks)].reshape(len(ks) * inner.shape[1], inner.shape[2])


WHOLE = [(z_at, y_at) for z_at in range(3) for y_at in range(3)]
LATE = [(3, 0), (3, 1), (3, 2), (0, 3), (1, 3), (2, 3), (3, 3)]


def late_ks(z_at, y_at):
    return ((0, 1) if z_at == 3 else ()) + ((2, 3) if y_at == 3 else ())


def spread(total):
    return jnp.broadcast_to(jnp.sum(total, keepdims=True), (1, 128))


def inner_kernel(sector, terms, sources, sizes, wave, right, masked, right_live, inner, sums):
    size = inner.shape[-1]
    me = sector[0]
    rows = lax.broadcasted_iota(jnp.int32, (size, size), 0)
    col_keep = lax.broadcasted_iota(jnp.int32, (size, size), 1) < sizes[0, 1, me]

    def mask_right(t, carry):
        right_live[t] = jnp.where(col_keep, right[0, t, 0].astype(jnp.float32), 0.0).astype(jnp.bfloat16)
        return carry

    def mask_wave(c, ww):
        keep = (rows < sizes[0, 0, c]) & col_keep
        w = jnp.where(keep, wave[0, c, 0].astype(jnp.float32), 0.0)
        masked[c] = w.astype(jnp.bfloat16)
        return ww + fold(w * w)

    lax.fori_loop(0, right_live.shape[0], mask_right, 0)
    ww = lax.fori_loop(0, masked.shape[0], mask_wave, jnp.zeros((8, size), jnp.float32))
    for z_at in range(4):
        for y_at in range(4):
            a = left_sector(me, z_at, y_at)
            for k in range(4):
                inner[4 * (4 * z_at + y_at) + k] = inner_product(a, k, terms, sources, masked, right_live)
    sums[...] = jnp.broadcast_to(spread(ww), sums.shape)


def first_kernel(sector, masked, inner, sums_wave, *refs):
    pieces, (field, part, sums), (image,) = refs[:12], refs[12:15], refs[15:]
    size = image.shape[-1]
    me = sector[0]
    zero = jnp.zeros((8, size), jnp.float32)
    some_ww, some_wy = zero, zero
    for i, (z_at, y_at) in enumerate(WHOLE):
        ks = (0, 1, 2, 3)
        y = dot(left_row(pieces, z_at, y_at, ks), inner_rows(inner, z_at, y_at, ks))
        image[i] = y
        w = masked[left_sector(me, z_at, y_at)].astype(jnp.float32)
        some_ww += fold(w * w)
        some_wy += fold(w * y)
    for i, (z_at, y_at) in enumerate(LATE[:6]):
        ks = (2, 3) if z_at == 3 else (0, 1)
        part[i] = dot(left_row(pieces, z_at, y_at, ks), inner_rows(inner, z_at, y_at, ks))

    some_ww = jnp.sum(some_ww, keepdims=True)
    some_wy = jnp.sum(some_wy, keepdims=True)
    slope = jnp.where(some_ww > 0.0, some_wy / jnp.where(some_ww > 0.0, some_ww, 1.0), 0.0)
    wu, uu = zero, zero
    for i, (z_at, y_at) in enumerate(WHOLE):
        w = masked[left_sector(me, z_at, y_at)].astype(jnp.float32)
        u = (image[i] - slope * w).astype(jnp.bfloat16)
        field[i] = u
        u = u.astype(jnp.float32)
        wu += fold(w * u)
        uu += fold(u * u)
    slope = jnp.broadcast_to(slope, (1, 128))
    sums[...] = jnp.concatenate([sums_wave[0:1], spread(wu), spread(uu)] + [slope] * 5, axis=0)


def second_kernel(sector, terms, sources, masked, right_live, field_some, part, inner, sums_first, *refs):
    pieces, (field, image, sums) = refs[:16], refs[16:]
    size = image.shape[-1]
    me = sector[0]
    zero = jnp.zeros((8, size), jnp.float32)
    slope = sums_first[3:4, :1]
    wu, uu = zero, zero
    for i, (z_at, y_at) in enumerate(LATE):
        a = left_sector(me, z_at, y_at)
        ks = late_ks(z_at, y_at)
        y = dot(left_row(pieces, z_at, y_at, ks), inner_rows(inner, z_at, y_at, ks))
        if i < 6:
            y += part[i]
        w = masked[a].astype(jnp.float32)
        u = (y - slope * w).astype(jnp.bfloat16)
        field[a] = u
        u = u.astype(jnp.float32)
        wu += fold(w * u)
        uu += fold(u * u)
    for i, (z_at, y_at) in enumerate(WHOLE):
        field[left_sector(me, z_at, y_at)] = field_some[i]

    wv, uv, vv = zero, zero, zero
    for z_at in range(4):
        for y_at in range(4):
            a = left_sector(me, z_at, y_at)
            v = row_image(a, z_at, y_at, terms, sources, field, right_live, pieces)
            image[a] = v
            wv += fold(masked[a].astype(jnp.float32) * v)
            uv += fold(field[a].astype(jnp.float32) * v)
            vv += fold(v * v)

    head = sums_first[...]
    block = jnp.concatenate(
        [
            head[0:1],
            head[1:2] + spread(wu),
            head[2:3] + spread(uu),
            spread(wv),
            spread(uv),
            spread(vv),
            head[3:4],
            head[3:4],
        ],
        axis=0,
    )
    sums[...] = jnp.broadcast_to(block[None], sums.shape)


def last_kernel(cells, gathered, own, masked, field, image, out, projected, weights):
    step = pl.program_id(0)

    @pl.when(step == 0)
    def _():
        g = gathered[...]
        ww, wu, uu, wv, uv, vv, slope = (g[:, j, :] for j in range(7))

        def total(values):
            return jnp.sum(values, axis=0, keepdims=True) / cells

        alpha = lax.rsqrt(total(ww) + epsilon)
        wy = wu + slope * ww
        uy = uu + slope * wu
        theta = alpha * alpha * total(wy)
        delta = theta - slope
        beta = lax.rsqrt(alpha * alpha * total(uu - 2.0 * delta * wu + delta * delta * ww) + epsilon)
        scale = alpha * beta
        upper = alpha * scale * total(wv - delta * wy)
        lower = scale * scale * total(uv - delta * uy - delta * (wv - delta * wy))
        cu = delta + lower
        cw = delta * slope - lower * delta + upper / beta
        squares = vv + cu * cu * uu + cw * cw * ww - 2.0 * (cu * uv + cw * wv - cu * cw * wu)
        gamma = lax.rsqrt(scale * scale * total(squares) + epsilon)
        factor = gamma * scale
        own_slope = own[0, 6:7, :]
        own_delta = theta - own_slope
        own_cu = own_delta + lower
        own_cw = own_delta * own_slope - lower * own_delta + upper / beta
        weights[...] = jnp.concatenate([factor, factor * own_cu, factor * own_cw], axis=0)
        lane = lax.broadcasted_iota(jnp.int32, theta.shape, 1)
        entries = jnp.where(lane == 0, theta, jnp.where(lane == 1, upper, lower))
        projected[...] = entries[:, :3]

    def wide(j):
        row = weights[j : j + 1, :]
        return jnp.concatenate([row] * (out.shape[-1] // 128), axis=1)[None]

    per_step = out.shape[1]
    here = pl.ds(step * per_step, per_step)
    out[0, :, 0] = (
        image[here] * wide(0)
        - field[here].astype(jnp.float32) * wide(1)
        - masked[here].astype(jnp.float32) * wide(2)
    )


def per_device(wavefunction, left_env, right_env, term_table, source_table, live_sizes):
    sectors, size = wavefunction.shape[1], wavefunction.shape[3]
    terms_count = left_env.shape[1]
    smem = pl.BlockSpec(memory_space=pltpu.SMEM)
    vmem = pl.BlockSpec(memory_space=pltpu.VMEM)
    bf16, f32 = jnp.bfloat16, jnp.float32
    sector = lax.axis_index("sector").astype(jnp.int32)[None]
    terms, sources = term_table.T, source_table.T

    def blocks(count, dtype):
        return jax.ShapeDtypeStruct((count, size, size), dtype)

    half_a, half_b = pl.pallas_call(
        pick_kernel,
        out_shape=(blocks(2, bf16), blocks(2, bf16)),
        in_specs=[smem, smem, smem, pl.BlockSpec(memory_space=pltpu.HBM)],
        out_specs=(vmem, vmem),
        scratch_shapes=[pltpu.VMEM((4, size, size), bf16), pltpu.SemaphoreType.DMA((4,))],
        compiler_params=pltpu.CompilerParams(vmem_limit_bytes=60 * MIB),
        name="pick_left",
    )(sector, terms, live_sizes, left_env)

    stage_a, stage_b = pl.pallas_call(
        stage_kernel,
        out_shape=(blocks(2, bf16), blocks(2, bf16)),
        in_specs=[vmem, vmem],
        out_specs=(vmem, vmem),
        compiler_params=pltpu.CompilerParams(vmem_limit_bytes=4 * MIB),
        cost_estimate=pl.CostEstimate(flops=1 << 20, bytes_accessed=MIB, transcendentals=0),
        name="stage",
    )(half_a, half_b)
    count = lax.axis_size("section")
    partner = lax.ppermute(
        right_env, "section", [(s, s ^ 1) for s in range(count)]
    )

    flop = 2 * size * size * size
    row = jax.ShapeDtypeStruct((8, 128), f32)
    masked, right_live, inner, sums_wave = pl.pallas_call(
        inner_kernel,
        out_shape=(blocks(sectors, bf16), blocks(terms_count, bf16), blocks(4 * sectors, bf16), row),
        in_specs=[smem] * 4 + [vmem] * 2,
        out_specs=(vmem,) * 4,
        compiler_params=pltpu.CompilerParams(vmem_limit_bytes=16 * MIB),
        cost_estimate=pl.CostEstimate(flops=64 * flop, bytes_accessed=12 * MIB, transcendentals=0),
        name="inner_products",
    )(sector, terms, sources, live_sizes, wavefunction, partner)

    pieces_a, pieces_b = gather_halves(half_a, half_b, stage_a, stage_b, sums_wave)
    early = pieces_a[:6] + pieces_b[:6]
    every = pieces_a + pieces_b
    field_some, part, sums_first = pl.pallas_call(
        first_kernel,
        out_shape=(blocks(len(WHOLE), bf16), blocks(6, f32), row),
        in_specs=[smem] + [vmem] * 15,
        out_specs=(vmem,) * 3,
        scratch_shapes=[pltpu.VMEM((len(WHOLE), size, size), f32)],
        compiler_params=pltpu.CompilerParams(vmem_limit_bytes=12 * MIB),
        name="first_image",
    )(sector, masked, inner, sums_wave, *early)

    field, image, sums = pl.pallas_call(
        second_kernel,
        out_shape=(
            blocks(sectors, bf16),
            blocks(sectors, f32),
            jax.ShapeDtypeStruct((sectors, 8, 128), f32),
        ),
        in_specs=[smem] * 3 + [vmem] * 22,
        out_specs=(vmem,) * 3,
        compiler_params=pltpu.CompilerParams(vmem_limit_bytes=20 * MIB),
        cost_estimate=pl.CostEstimate(flops=144 * flop, bytes_accessed=24 * MIB, transcendentals=0),
        name="second_image",
    )(sector, terms, sources, masked, right_live, field_some, part, inner, sums_first, *every)

    gathered = lax.all_to_all(sums, "sector", 0, 0)
    per_step = 8
    cells = float(sectors * sectors * size * size)
    next_basis, projected = pl.pallas_call(
        functools.partial(last_kernel, cells),
        grid=(sectors // per_step,),
        out_shape=(
            jax.ShapeDtypeStruct((1, sectors, 1, size, size), f32),
            jax.ShapeDtypeStruct((1, 3), f32),
        ),
        in_specs=[vmem] * 5,
        out_specs=(
            pl.BlockSpec((1, per_step, 1, size, size), lambda i: (0, i, 0, 0, 0)),
            pl.BlockSpec((1, 3), lambda i: (0, 0)),
        ),
        scratch_shapes=[pltpu.VMEM((3, 128), f32)],
        compiler_params=pltpu.CompilerParams(vmem_limit_bytes=12 * MIB),
        name="next_basis",
    )(gathered, sums, masked, field, image)
    return next_basis, projected


def solution(mesh):
    in_specs = (
        P("section", None, "sector", None, None),
        P("section", None, "sector", None, None),
        P("section", None, "sector", None, None),
        P(),
        P(),
        P("section", None, None),
    )
    out_specs = (P("section", None, "sector", None, None), P("section", None))
    return jax.shard_map(
        per_device, mesh=mesh, in_specs=in_specs, out_specs=out_specs, check_vma=False
    )
```

```python
import functools

import jax
import jax.numpy as jnp
from jax import lax
from jax.experimental import pallas as pl
from jax.experimental.pallas import tpu as pltpu
from jax.sharding import PartitionSpec as P

epsilon = 1e-06
SIDE = 4
OFFSETS = (0, 3, 1, 2)
MIB = 1 << 20


def ring(dz, dy):
    return [
        (z * SIDE + y, ((z + dz) % SIDE) * SIDE + (y + dy) % SIDE)
        for z in range(SIDE)
        for y in range(SIDE)
    ]


def along(axis, step):
    return ring(step % SIDE, 0) if axis == "z" else ring(0, step % SIDE)


def send(block, axis, step):
    return lax.ppermute(block, "sector", along(axis, step))


def after(value, *results):
    return lax.optimization_barrier((value, *results))[0]


def gather_halves(half_a, half_b, stage_a, stage_b, gate):
    own, kept = (half_a, half_b), (stage_a, stage_b)
    first, second = ("y", "z"), ("z", "y")
    near = {(i, step): send(own[i], first[i], step) for i in range(2) for step in (1, -1)}
    across = [send(near[i, 1], first[i], 1) for i in range(2)]
    last = {(first[i], step): near[i, step] for i in range(2) for step in (1, -1)}
    last.update({(first[i], 1): across[i] for i in range(2)})
    low = [jnp.stack([kept[i], near[i, 1]]) for i in range(2)]
    high = [jnp.stack([near[i, -1], across[i]]) for i in range(2)]
    low_next, high_next = {}, {}
    for i in range(2):
        for step in (1, -1):
            low_next[i, step] = send(after(low[i], last[second[i], step]), second[i], step)
    for i in range(2):
        for step in (1, -1):
            high_next[i, step] = send(after(high[i], low_next[i, step]), second[i], step)
    pieces = []
    for i in range(2):
        one, two = low_next[i, 1], low_next[i, -1]
        up = one[1]
        down = jnp.concatenate([high_next[i, -1].reshape(4, *two.shape[2:]), two[0]])
        pieces.append(
            [
                low[i],
                high[i],
                low_next[i, 1],
                high_next[i, 1],
                low_next[i, -1],
                high_next[i, -1],
                send(after(up, high_next[i, 1], gate), second[i], 1),
                send(down, second[i], -1),
            ]
        )
    return pieces


def left_sector(sector, z_at, y_at):
    z = lax.rem(sector // SIDE + OFFSETS[z_at], SIDE)
    y = lax.rem(lax.rem(sector, SIDE) + OFFSETS[y_at], SIDE)
    return z * SIDE + y


def fold(block):
    return jnp.sum(block.reshape(block.shape[0] // 8, 8, block.shape[1]), axis=0)


def dot(a, b):
    return jnp.dot(a, b, preferred_element_type=jnp.float32)


def pick_kernel(sector, terms, sizes, left, half_a, half_b, blocks, sems):
    me = sector[0]
    copies = [pltpu.make_async_copy(left.at[0, terms[k, me], 0], blocks.at[k], sems.at[k]) for k in range(4)]
    for copy in copies:
        copy.start()
    size = blocks.shape[-1]
    keep = lax.broadcasted_iota(jnp.int32, (size, size), 0) < sizes[0, 0, me]
    for k, copy in enumerate(copies):
        copy.wait()
        block = jnp.where(keep, blocks[k].astype(jnp.float32), 0.0).astype(jnp.bfloat16)
        (half_a, half_b)[k // 2][k % 2] = block


def stage_kernel(half_a, half_b, stage_a, stage_b):
    stage_a[...] = half_a[...]
    stage_b[...] = half_b[...]


def inner_product(a, k, terms, sources, vector, right):
    return dot(vector[sources[k, a]], right[terms[k, a]]).astype(jnp.bfloat16)


ACROSS = (((7, 4), (7, 5)), ((6, 0), (6, 1)), ((7, 0), (7, 1)), ((7, 2), (7, 3)))


def left_block(pieces, z_at, y_at, k):
    half = k // 2
    first_at, second_at = ((y_at, z_at), (z_at, y_at))[half]
    of_half = pieces[len(pieces) // 2 * half :]
    if second_at == 3:
        array, entry = ACROSS[first_at][k % 2]
        return of_half[array][entry]
    return of_half[2 * second_at + first_at // 2][first_at % 2, k % 2]


def left_row(pieces, z_at, y_at, ks):
    return jnp.concatenate([left_block(pieces, z_at, y_at, k) for k in ks], axis=1)


def row_image(a, z_at, y_at, terms, sources, vector, right, pieces):
    inner = [inner_product(a, k, terms, sources, vector, right) for k in range(4)]
    return dot(left_row(pieces, z_at, y_at, range(4)), jnp.concatenate(inner, axis=0))


def inner_rows(inner, z_at, y_at, ks):
    at = 4 * (4 * z_at + y_at) + ks[0]
    return inner[at : at + len(ks)].reshape(len(ks) * inner.shape[1], inner.shape[2])


WHOLE = [(z_at, y_at) for z_at in range(3) for y_at in range(3)]
LATE = [(3, 0), (3, 1), (3, 2), (0, 3), (1, 3), (2, 3), (3, 3)]


def late_ks(z_at, y_at):
    return ((0, 1) if z_at == 3 else ()) + ((2, 3) if y_at == 3 else ())


def spread(total):
    return jnp.broadcast_to(jnp.sum(total, keepdims=True), (1, 128))


def inner_kernel(sector, terms, sources, sizes, wave, right, masked, right_live, inner, sums):
    size = inner.shape[-1]
    me = sector[0]
    rows = lax.broadcasted_iota(jnp.int32, (size, size), 0)
    col_keep = lax.broadcasted_iota(jnp.int32, (size, size), 1) < sizes[0, 1, me]

    def mask_right(t, carry):
        right_live[t] = jnp.where(col_keep, right[0, t, 0].astype(jnp.float32), 0.0).astype(jnp.bfloat16)
        return carry

    def mask_wave(c, ww):
        keep = (rows < sizes[0, 0, c]) & col_keep
        w = jnp.where(keep, wave[0, c, 0].astype(jnp.float32), 0.0)
        masked[c] = w.astype(jnp.bfloat16)
        return ww + fold(w * w)

    lax.fori_loop(0, right_live.shape[0], mask_right, 0)
    ww = lax.fori_loop(0, masked.shape[0], mask_wave, jnp.zeros((8, size), jnp.float32))
    for z_at in range(4):
        for y_at in range(4):
            a = left_sector(me, z_at, y_at)
            for k in range(4):
                inner[4 * (4 * z_at + y_at) + k] = inner_product(a, k, terms, sources, masked, right_live)
    sums[...] = jnp.broadcast_to(spread(ww), sums.shape)


def first_kernel(sector, masked, inner, sums_wave, *refs):
    pieces, (field, part, sums), (image,) = refs[:12], refs[12:15], refs[15:]
    size = image.shape[-1]
    me = sector[0]
    zero = jnp.zeros((8, size), jnp.float32)
    some_ww, some_wy = zero, zero
    for i, (z_at, y_at) in enumerate(WHOLE):
        ks = (0, 1, 2, 3)
        y = dot(left_row(pieces, z_at, y_at, ks), inner_rows(inner, z_at, y_at, ks))
        image[i] = y
        w = masked[left_sector(me, z_at, y_at)].astype(jnp.float32)
        some_ww += fold(w * w)
        some_wy += fold(w * y)
    for i, (z_at, y_at) in enumerate(LATE[:6]):
        ks = (2, 3) if z_at == 3 else (0, 1)
        part[i] = dot(left_row(pieces, z_at, y_at, ks), inner_rows(inner, z_at, y_at, ks))

    some_ww = jnp.sum(some_ww, keepdims=True)
    some_wy = jnp.sum(some_wy, keepdims=True)
    usable = some_ww > 1e-30
    slope = jnp.where(usable, some_wy / jnp.where(usable, some_ww, 1.0), 0.0)
    wu, uu = zero, zero
    for i, (z_at, y_at) in enumerate(WHOLE):
        w = masked[left_sector(me, z_at, y_at)].astype(jnp.float32)
        u = (image[i] - slope * w).astype(jnp.bfloat16)
        field[i] = u
        u = u.astype(jnp.float32)
        wu += fold(w * u)
        uu += fold(u * u)
    slope = jnp.broadcast_to(slope, (1, 128))
    sums[...] = jnp.concatenate([sums_wave[0:1], spread(wu), spread(uu)] + [slope] * 5, axis=0)


def second_kernel(sector, terms, sources, masked, right_live, field_some, part, inner, sums_first, *refs):
    pieces, (field, image, sums) = refs[:16], refs[16:]
    size = image.shape[-1]
    me = sector[0]
    zero = jnp.zeros((8, size), jnp.float32)
    slope = sums_first[3:4, :1]
    wu, uu = zero, zero
    for i, (z_at, y_at) in enumerate(LATE):
        a = left_sector(me, z_at, y_at)
        ks = late_ks(z_at, y_at)
        y = dot(left_row(pieces, z_at, y_at, ks), inner_rows(inner, z_at, y_at, ks))
        if i < 6:
            y += part[i]
        w = masked[a].astype(jnp.float32)
        u = (y - slope * w).astype(jnp.bfloat16)
        field[a] = u
        u = u.astype(jnp.float32)
        wu += fold(w * u)
        uu += fold(u * u)
    for i, (z_at, y_at) in enumerate(WHOLE):
        field[left_sector(me, z_at, y_at)] = field_some[i]

    wv, uv, vv = zero, zero, zero
    for z_at in range(4):
        for y_at in range(4):
            a = left_sector(me, z_at, y_at)
            v = row_image(a, z_at, y_at, terms, sources, field, right_live, pieces)
            image[a] = v
            wv += fold(masked[a].astype(jnp.float32) * v)
            uv += fold(field[a].astype(jnp.float32) * v)
            vv += fold(v * v)

    head = sums_first[...]
    block = jnp.concatenate(
        [
            head[0:1],
            head[1:2] + spread(wu),
            head[2:3] + spread(uu),
            spread(wv),
            spread(uv),
            spread(vv),
            head[3:4],
            head[3:4],
        ],
        axis=0,
    )
    sums[...] = jnp.broadcast_to(block[None], sums.shape)


def last_kernel(cells, gathered, own, masked, field, image, out, projected, weights):
    step = pl.program_id(0)

    @pl.when(step == 0)
    def _():
        g = gathered[...]
        ww, wu, uu, wv, uv, vv, slope = (g[:, j, :] for j in range(7))

        def total(values):
            return jnp.sum(values, axis=0, keepdims=True) / cells

        alpha = lax.rsqrt(total(ww) + epsilon)
        wy = wu + slope * ww
        uy = uu + slope * wu
        theta = alpha * alpha * total(wy)
        delta = theta - slope
        rest = total(uu - 2.0 * delta * wu + delta * delta * ww)
        beta = lax.rsqrt(alpha * alpha * jnp.maximum(rest, 0.0) + epsilon)
        scale = alpha * beta
        upper = alpha * scale * total(wv - delta * wy)
        lower = scale * scale * total(uv - delta * uy - delta * (wv - delta * wy))
        cu = delta + lower
        cw = delta * slope - lower * delta + upper / beta
        squares = vv + cu * cu * uu + cw * cw * ww - 2.0 * (cu * uv + cw * wv - cu * cw * wu)
        gamma = lax.rsqrt(scale * scale * jnp.maximum(total(squares), 0.0) + epsilon)
        factor = gamma * scale
        own_slope = own[0, 6:7, :]
        own_delta = theta - own_slope
        own_cu = own_delta + lower
        own_cw = own_delta * own_slope - lower * own_delta + upper / beta
        weights[...] = jnp.concatenate([factor, factor * own_cu, factor * own_cw], axis=0)
        lane = lax.broadcasted_iota(jnp.int32, theta.shape, 1)
        entries = jnp.where(lane == 0, theta, jnp.where(lane == 1, upper, lower))
        projected[...] = entries[:, :3]

    def wide(j):
        row = weights[j : j + 1, :]
        return jnp.concatenate([row] * (out.shape[-1] // 128), axis=1)[None]

    per_step = out.shape[1]
    here = pl.ds(step * per_step, per_step)
    out[0, :, 0] = (
        image[here] * wide(0)
        - field[here].astype(jnp.float32) * wide(1)
        - masked[here].astype(jnp.float32) * wide(2)
    )


def per_device(wavefunction, left_env, right_env, term_table, source_table, live_sizes):
    sectors, size = wavefunction.shape[1], wavefunction.shape[3]
    terms_count = left_env.shape[1]
    smem = pl.BlockSpec(memory_space=pltpu.SMEM)
    vmem = pl.BlockSpec(memory_space=pltpu.VMEM)
    bf16, f32 = jnp.bfloat16, jnp.float32
    sector = lax.axis_index("sector").astype(jnp.int32)[None]
    terms, sources = term_table.T, source_table.T

    def blocks(count, dtype):
        return jax.ShapeDtypeStruct((count, size, size), dtype)

    half_a, half_b = pl.pallas_call(
        pick_kernel,
        out_shape=(blocks(2, bf16), blocks(2, bf16)),
        in_specs=[smem, smem, smem, pl.BlockSpec(memory_space=pltpu.HBM)],
        out_specs=(vmem, vmem),
        scratch_shapes=[pltpu.VMEM((4, size, size), bf16), pltpu.SemaphoreType.DMA((4,))],
        compiler_params=pltpu.CompilerParams(vmem_limit_bytes=60 * MIB),
        name="pick_left",
    )(sector, terms, live_sizes, left_env)

    stage_a, stage_b = pl.pallas_call(
        stage_kernel,
        out_shape=(blocks(2, bf16), blocks(2, bf16)),
        in_specs=[vmem, vmem],
        out_specs=(vmem, vmem),
        compiler_params=pltpu.CompilerParams(vmem_limit_bytes=4 * MIB),
        cost_estimate=pl.CostEstimate(flops=1 << 20, bytes_accessed=MIB, transcendentals=0),
        name="stage",
    )(half_a, half_b)
    count = lax.axis_size("section")
    partner = lax.ppermute(
        right_env, "section", [(s, s ^ 1) for s in range(count)]
    )

    flop = 2 * size * size * size
    row = jax.ShapeDtypeStruct((8, 128), f32)
    masked, right_live, inner, sums_wave = pl.pallas_call(
        inner_kernel,
        out_shape=(blocks(sectors, bf16), blocks(terms_count, bf16), blocks(4 * sectors, bf16), row),
        in_specs=[smem] * 4 + [vmem] * 2,
        out_specs=(vmem,) * 4,
        compiler_params=pltpu.CompilerParams(vmem_limit_bytes=16 * MIB),
        cost_estimate=pl.CostEstimate(flops=64 * flop, bytes_accessed=12 * MIB, transcendentals=0),
        name="inner_products",
    )(sector, terms, sources, live_sizes, wavefunction, partner)

    pieces_a, pieces_b = gather_halves(half_a, half_b, stage_a, stage_b, sums_wave)
    early = pieces_a[:6] + pieces_b[:6]
    every = pieces_a + pieces_b
    field_some, part, sums_first = pl.pallas_call(
        first_kernel,
        out_shape=(blocks(len(WHOLE), bf16), blocks(6, f32), row),
        in_specs=[smem] + [vmem] * 15,
        out_specs=(vmem,) * 3,
        scratch_shapes=[pltpu.VMEM((len(WHOLE), size, size), f32)],
        compiler_params=pltpu.CompilerParams(vmem_limit_bytes=12 * MIB),
        name="first_image",
    )(sector, masked, inner, sums_wave, *early)

    field, image, sums = pl.pallas_call(
        second_kernel,
        out_shape=(
            blocks(sectors, bf16),
            blocks(sectors, f32),
            jax.ShapeDtypeStruct((sectors, 8, 128), f32),
        ),
        in_specs=[smem] * 3 + [vmem] * 22,
        out_specs=(vmem,) * 3,
        compiler_params=pltpu.CompilerParams(vmem_limit_bytes=20 * MIB),
        cost_estimate=pl.CostEstimate(flops=144 * flop, bytes_accessed=24 * MIB, transcendentals=0),
        name="second_image",
    )(sector, terms, sources, masked, right_live, field_some, part, inner, sums_first, *every)

    gathered = lax.all_to_all(sums, "sector", 0, 0)
    per_step = 8
    cells = float(sectors * sectors * size * size)
    next_basis, projected = pl.pallas_call(
        functools.partial(last_kernel, cells),
        grid=(sectors // per_step,),
        out_shape=(
            jax.ShapeDtypeStruct((1, sectors, 1, size, size), f32),
            jax.ShapeDtypeStruct((1, 3), f32),
        ),
        in_specs=[vmem] * 5,
        out_specs=(
            pl.BlockSpec((1, per_step, 1, size, size), lambda i: (0, i, 0, 0, 0)),
            pl.BlockSpec((1, 3), lambda i: (0, 0)),
        ),
        scratch_shapes=[pltpu.VMEM((3, 128), f32)],
        compiler_params=pltpu.CompilerParams(vmem_limit_bytes=12 * MIB),
        name="next_basis",
    )(gathered, sums, masked, field, image)
    return next_basis, projected


def solution(mesh):
    in_specs = (
        P("section", None, "sector", None, None),
        P("section", None, "sector", None, None),
        P("section", None, "sector", None, None),
        P(),
        P(),
        P("section", None, None),
    )
    out_specs = (P("section", None, "sector", None, None), P("section", None))
    return jax.shard_map(
        per_device, mesh=mesh, in_specs=in_specs, out_specs=out_specs, check_vma=False
    )
```

```python
import functools

import jax
import jax.numpy as jnp
from jax import lax
from jax.experimental import pallas as pl
from jax.experimental.pallas import tpu as pltpu
from jax.sharding import PartitionSpec as P

epsilon = 1e-06
SIDE = 4
OFFSETS = (0, 3, 1, 2)
MIB = 1 << 20


def ring(dz, dy):
    return [
        (z * SIDE + y, ((z + dz) % SIDE) * SIDE + (y + dy) % SIDE)
        for z in range(SIDE)
        for y in range(SIDE)
    ]


def along(axis, step):
    return ring(step % SIDE, 0) if axis == "z" else ring(0, step % SIDE)


def send(block, axis, step):
    return lax.ppermute(block, "sector", along(axis, step))


def after(value, *results):
    return lax.optimization_barrier((value, *results))[0]


def gather_halves(half_a, half_b, stage_a, stage_b, gate):
    own, kept = (half_a, half_b), (stage_a, stage_b)
    first, second = ("y", "z"), ("z", "y")
    near = {(i, step): send(own[i], first[i], step) for i in range(2) for step in (1, -1)}
    across = [send(near[i, 1], first[i], 1) for i in range(2)]
    last = {(first[i], step): near[i, step] for i in range(2) for step in (1, -1)}
    last.update({(first[i], 1): across[i] for i in range(2)})
    low = [jnp.stack([kept[i], near[i, 1]]) for i in range(2)]
    high = [jnp.stack([near[i, -1], across[i]]) for i in range(2)]
    low_next, high_next = {}, {}
    for i in range(2):
        for step in (1, -1):
            low_next[i, step] = send(after(low[i], last[second[i], step]), second[i], step)
    for i in range(2):
        for step in (1, -1):
            high_next[i, step] = send(after(high[i], low_next[i, step]), second[i], step)
    pieces = []
    for i in range(2):
        one, two = low_next[i, 1], low_next[i, -1]
        up = one[1]
        down = jnp.concatenate([high_next[i, -1].reshape(4, *two.shape[2:]), two[0]])
        pieces.append(
            [
                low[i],
                high[i],
                low_next[i, 1],
                high_next[i, 1],
                low_next[i, -1],
                high_next[i, -1],
                send(after(up, high_next[i, 1], gate), second[i], 1),
                send(down, second[i], -1),
            ]
        )
    return pieces


def left_sector(sector, z_at, y_at):
    z = lax.rem(sector // SIDE + OFFSETS[z_at], SIDE)
    y = lax.rem(lax.rem(sector, SIDE) + OFFSETS[y_at], SIDE)
    return z * SIDE + y


def fold(block):
    return jnp.sum(block.reshape(block.shape[0] // 8, 8, block.shape[1]), axis=0)


def dot(a, b):
    return jnp.dot(a, b, preferred_element_type=jnp.float32)


def pick_kernel(sector, terms, sizes, left, half_a, half_b, blocks, sems):
    me = sector[0]
    copies = [pltpu.make_async_copy(left.at[0, terms[k, me], 0], blocks.at[k], sems.at[k]) for k in range(4)]
    for copy in copies:
        copy.start()
    size = blocks.shape[-1]
    keep = lax.broadcasted_iota(jnp.int32, (size, size), 0) < sizes[0, 0, me]
    for k, copy in enumerate(copies):
        copy.wait()
        block = jnp.where(keep, blocks[k].astype(jnp.float32), 0.0).astype(jnp.bfloat16)
        (half_a, half_b)[k // 2][k % 2] = block


def stage_kernel(half_a, half_b, stage_a, stage_b):
    stage_a[...] = half_a[...]
    stage_b[...] = half_b[...]


def inner_product(a, k, terms, sources, vector, right):
    return dot(vector[sources[k, a]], right[terms[k, a]]).astype(jnp.bfloat16)


ACROSS = (((7, 4), (7, 5)), ((6, 0), (6, 1)), ((7, 0), (7, 1)), ((7, 2), (7, 3)))


def left_block(pieces, z_at, y_at, k):
    half = k // 2
    first_at, second_at = ((y_at, z_at), (z_at, y_at))[half]
    of_half = pieces[len(pieces) // 2 * half :]
    if second_at == 3:
        array, entry = ACROSS[first_at][k % 2]
        return of_half[array][entry]
    return of_half[2 * second_at + first_at // 2][first_at % 2, k % 2]


def left_row(pieces, z_at, y_at, ks):
    return jnp.concatenate([left_block(pieces, z_at, y_at, k) for k in ks], axis=1)


def row_image(a, z_at, y_at, terms, sources, vector, right, pieces):
    inner = [inner_product(a, k, terms, sources, vector, right) for k in range(4)]
    return dot(left_row(pieces, z_at, y_at, range(4)), jnp.concatenate(inner, axis=0))


def inner_rows(inner, z_at, y_at, ks):
    at = 4 * (4 * z_at + y_at) + ks[0]
    return inner[at : at + len(ks)].reshape(len(ks) * inner.shape[1], inner.shape[2])


WHOLE = [(z_at, y_at) for z_at in range(3) for y_at in range(3)]
LATE = [(3, 0), (3, 1), (3, 2), (0, 3), (1, 3), (2, 3), (3, 3)]


def late_ks(z_at, y_at):
    return ((0, 1) if z_at == 3 else ()) + ((2, 3) if y_at == 3 else ())


def spread(total):
    return jnp.broadcast_to(jnp.sum(total, keepdims=True), (1, 128))


def inner_kernel(sector, terms, sources, sizes, wave, right, masked, right_live, inner, sums):
    size = inner.shape[-1]
    me = sector[0]
    rows = lax.broadcasted_iota(jnp.int32, (size, size), 0)
    col_keep = lax.broadcasted_iota(jnp.int32, (size, size), 1) < sizes[0, 1, me]

    def mask_right(t, carry):
        right_live[t] = jnp.where(col_keep, right[0, t, 0].astype(jnp.float32), 0.0).astype(jnp.bfloat16)
        return carry

    def mask_wave(c, ww):
        keep = (rows < sizes[0, 0, c]) & col_keep
        w = jnp.where(keep, wave[0, c, 0].astype(jnp.float32), 0.0)
        masked[c] = w.astype(jnp.bfloat16)
        return ww + fold(w * w)

    lax.fori_loop(0, right_live.shape[0], mask_right, 0)
    ww = lax.fori_loop(0, masked.shape[0], mask_wave, jnp.zeros((8, size), jnp.float32))
    for z_at in range(4):
        for y_at in range(4):
            a = left_sector(me, z_at, y_at)
            for k in range(4):
                inner[4 * (4 * z_at + y_at) + k] = inner_product(a, k, terms, sources, masked, right_live)
    sums[...] = jnp.broadcast_to(spread(ww), sums.shape)


def first_kernel(sector, masked, inner, sums_wave, *refs):
    pieces, (field, part, sums), (image,) = refs[:12], refs[12:15], refs[15:]
    size = image.shape[-1]
    me = sector[0]
    zero = jnp.zeros((8, size), jnp.float32)
    some_ww, some_wy = zero, zero
    for i, (z_at, y_at) in enumerate(WHOLE):
        ks = (0, 1, 2, 3)
        y = dot(left_row(pieces, z_at, y_at, ks), inner_rows(inner, z_at, y_at, ks))
        image[i] = y
        w = masked[left_sector(me, z_at, y_at)].astype(jnp.float32)
        some_ww += fold(w * w)
        some_wy += fold(w * y)
    for i, (z_at, y_at) in enumerate(LATE[:6]):
        ks = (2, 3) if z_at == 3 else (0, 1)
        part[i] = dot(left_row(pieces, z_at, y_at, ks), inner_rows(inner, z_at, y_at, ks))

    some_ww = jnp.sum(some_ww, keepdims=True)
    some_wy = jnp.sum(some_wy, keepdims=True)
    usable = some_ww > 1e-30
    slope = jnp.where(usable, some_wy / jnp.where(usable, some_ww, 1.0), 0.0)
    wu, uu = zero, zero
    for i, (z_at, y_at) in enumerate(WHOLE):
        w = masked[left_sector(me, z_at, y_at)].astype(jnp.float32)
        u = (image[i] - slope * w).astype(jnp.bfloat16)
        field[i] = u
        u = u.astype(jnp.float32)
        wu += fold(w * u)
        uu += fold(u * u)
    slope = jnp.broadcast_to(slope, (1, 128))
    sums[...] = jnp.concatenate([sums_wave[0:1], spread(wu), spread(uu)] + [slope] * 5, axis=0)


def second_kernel(sector, terms, sources, masked, right_live, field_some, part, inner, sums_first, *refs):
    pieces, (field, image, sums) = refs[:16], refs[16:]
    size = image.shape[-1]
    me = sector[0]
    zero = jnp.zeros((8, size), jnp.float32)
    slope = sums_first[3:4, :1]
    wu, uu = zero, zero
    for i, (z_at, y_at) in enumerate(LATE):
        a = left_sector(me, z_at, y_at)
        ks = late_ks(z_at, y_at)
        y = dot(left_row(pieces, z_at, y_at, ks), inner_rows(inner, z_at, y_at, ks))
        if i < 6:
            y += part[i]
        w = masked[a].astype(jnp.float32)
        u = (y - slope * w).astype(jnp.bfloat16)
        field[a] = u
        u = u.astype(jnp.float32)
        wu += fold(w * u)
        uu += fold(u * u)
    for i, (z_at, y_at) in enumerate(WHOLE):
        field[left_sector(me, z_at, y_at)] = field_some[i]

    wv, uv, vv = zero, zero, zero
    for z_at in range(4):
        for y_at in range(4):
            a = left_sector(me, z_at, y_at)
            v = row_image(a, z_at, y_at, terms, sources, field, right_live, pieces)
            image[a] = v
            wv += fold(masked[a].astype(jnp.float32) * v)
            uv += fold(field[a].astype(jnp.float32) * v)
            vv += fold(v * v)

    head = sums_first[...]
    block = jnp.concatenate(
        [
            head[0:1],
            head[1:2] + spread(wu),
            head[2:3] + spread(uu),
            spread(wv),
            spread(uv),
            spread(vv),
            head[3:4],
            head[3:4],
        ],
        axis=0,
    )
    sums[...] = jnp.broadcast_to(block[None], sums.shape)


def last_kernel(cells, gathered, own, masked, field, image, out, projected, weights, ready, sems):
    def weigh():
        g = gathered[...]
        ww, wu, uu, wv, uv, vv, slope = (g[:, j, :] for j in range(7))

        def total(values):
            return jnp.sum(values, axis=0, keepdims=True) / cells

        alpha = lax.rsqrt(total(ww) + epsilon)
        wy = wu + slope * ww
        uy = uu + slope * wu
        theta = alpha * alpha * total(wy)
        delta = theta - slope
        rest = total(uu - 2.0 * delta * wu + delta * delta * ww)
        beta = lax.rsqrt(alpha * alpha * jnp.maximum(rest, 0.0) + epsilon)
        scale = alpha * beta
        upper = alpha * scale * total(wv - delta * wy)
        lower = scale * scale * total(uv - delta * uy - delta * (wv - delta * wy))
        cu = delta + lower
        cw = delta * slope - lower * delta + upper / beta
        squares = vv + cu * cu * uu + cw * cw * ww - 2.0 * (cu * uv + cw * wv - cu * cw * wu)
        gamma = lax.rsqrt(scale * scale * jnp.maximum(total(squares), 0.0) + epsilon)
        factor = gamma * scale
        own_slope = own[0, 6:7, :]
        own_delta = theta - own_slope
        own_cu = own_delta + lower
        own_cw = own_delta * own_slope - lower * own_delta + upper / beta
        weights[...] = jnp.concatenate([factor, factor * own_cu, factor * own_cw], axis=0)
        lane = lax.broadcasted_iota(jnp.int32, theta.shape, 1)
        entries = jnp.where(lane == 0, theta, jnp.where(lane == 1, upper, lower))
        projected[...] = entries[:, :3]

    def wide(j):
        row = weights[j : j + 1, :]
        return jnp.concatenate([row] * (out.shape[-1] // 128), axis=1)[None]

    weigh()
    parts = sems.shape[0]
    per_part = ready.shape[0] // parts
    copies = []
    for part in range(parts):
        here = pl.ds(part * per_part, per_part)
        ready[here] = (
            image[here] * wide(0)
            - field[here].astype(jnp.float32) * wide(1)
            - masked[here].astype(jnp.float32) * wide(2)
        )
        copies.append(pltpu.make_async_copy(ready.at[here], out.at[0, here, 0], sems.at[part]))
        copies[-1].start()
    for copy in copies:
        copy.wait()


def per_device(wavefunction, left_env, right_env, term_table, source_table, live_sizes):
    sectors, size = wavefunction.shape[1], wavefunction.shape[3]
    terms_count = left_env.shape[1]
    smem = pl.BlockSpec(memory_space=pltpu.SMEM)
    vmem = pl.BlockSpec(memory_space=pltpu.VMEM)
    bf16, f32 = jnp.bfloat16, jnp.float32
    sector = lax.axis_index("sector").astype(jnp.int32)[None]
    terms, sources = term_table.T, source_table.T

    def blocks(count, dtype):
        return jax.ShapeDtypeStruct((count, size, size), dtype)

    half_a, half_b = pl.pallas_call(
        pick_kernel,
        out_shape=(blocks(2, bf16), blocks(2, bf16)),
        in_specs=[smem, smem, smem, pl.BlockSpec(memory_space=pltpu.HBM)],
        out_specs=(vmem, vmem),
        scratch_shapes=[pltpu.VMEM((4, size, size), bf16), pltpu.SemaphoreType.DMA((4,))],
        compiler_params=pltpu.CompilerParams(vmem_limit_bytes=60 * MIB),
        name="pick_left",
    )(sector, terms, live_sizes, left_env)

    stage_a, stage_b = pl.pallas_call(
        stage_kernel,
        out_shape=(blocks(2, bf16), blocks(2, bf16)),
        in_specs=[vmem, vmem],
        out_specs=(vmem, vmem),
        compiler_params=pltpu.CompilerParams(vmem_limit_bytes=4 * MIB),
        cost_estimate=pl.CostEstimate(flops=1 << 20, bytes_accessed=MIB, transcendentals=0),
        name="stage",
    )(half_a, half_b)
    count = lax.axis_size("section")
    partner = lax.ppermute(
        right_env, "section", [(s, s ^ 1) for s in range(count)]
    )

    flop = 2 * size * size * size
    row = jax.ShapeDtypeStruct((8, 128), f32)
    masked, right_live, inner, sums_wave = pl.pallas_call(
        inner_kernel,
        out_shape=(blocks(sectors, bf16), blocks(terms_count, bf16), blocks(4 * sectors, bf16), row),
        in_specs=[smem] * 4 + [vmem] * 2,
        out_specs=(vmem,) * 4,
        compiler_params=pltpu.CompilerParams(vmem_limit_bytes=16 * MIB),
        cost_estimate=pl.CostEstimate(flops=64 * flop, bytes_accessed=12 * MIB, transcendentals=0),
        name="inner_products",
    )(sector, terms, sources, live_sizes, wavefunction, partner)

    pieces_a, pieces_b = gather_halves(half_a, half_b, stage_a, stage_b, sums_wave)
    early = pieces_a[:6] + pieces_b[:6]
    every = pieces_a + pieces_b
    field_some, part, sums_first = pl.pallas_call(
        first_kernel,
        out_shape=(blocks(len(WHOLE), bf16), blocks(6, f32), row),
        in_specs=[smem] + [vmem] * 15,
        out_specs=(vmem,) * 3,
        scratch_shapes=[pltpu.VMEM((len(WHOLE), size, size), f32)],
        compiler_params=pltpu.CompilerParams(vmem_limit_bytes=12 * MIB),
        name="first_image",
    )(sector, masked, inner, sums_wave, *early)

    field, image, sums = pl.pallas_call(
        second_kernel,
        out_shape=(
            blocks(sectors, bf16),
            blocks(sectors, f32),
            jax.ShapeDtypeStruct((sectors, 8, 128), f32),
        ),
        in_specs=[smem] * 3 + [vmem] * 22,
        out_specs=(vmem,) * 3,
        compiler_params=pltpu.CompilerParams(vmem_limit_bytes=20 * MIB),
        cost_estimate=pl.CostEstimate(flops=144 * flop, bytes_accessed=24 * MIB, transcendentals=0),
        name="second_image",
    )(sector, terms, sources, masked, right_live, field_some, part, inner, sums_first, *every)

    gathered = lax.all_to_all(sums, "sector", 0, 0)
    cells = float(sectors * sectors * size * size)
    next_basis, projected = pl.pallas_call(
        functools.partial(last_kernel, cells),
        out_shape=(
            jax.ShapeDtypeStruct((1, sectors, 1, size, size), f32),
            jax.ShapeDtypeStruct((1, 3), f32),
        ),
        in_specs=[vmem] * 5,
        out_specs=(pl.BlockSpec(memory_space=pl.ANY), vmem),
        scratch_shapes=[
            pltpu.VMEM((3, 128), f32),
            pltpu.VMEM((sectors, size, size), f32),
            pltpu.SemaphoreType.DMA((8,)),
        ],
        compiler_params=pltpu.CompilerParams(vmem_limit_bytes=12 * MIB),
        name="next_basis",
    )(gathered, sums, masked, field, image)
    return next_basis, projected


def solution(mesh):
    in_specs = (
        P("section", None, "sector", None, None),
        P("section", None, "sector", None, None),
        P("section", None, "sector", None, None),
        P(),
        P(),
        P("section", None, None),
    )
    out_specs = (P("section", None, "sector", None, None), P("section", None))
    return jax.shard_map(
        per_device, mesh=mesh, in_specs=in_specs, out_specs=out_specs, check_vma=False
    )
```
